256 devices in a mesh: scan: 16 (over y, x), chan: 16 (over z, core).
Axes of the slice: x: 4, y: 4, z: 8, core: 2. Of those that a mesh axis runs over, the one named last changes fastest.
Arguments:
- spectra: bfloat16 [16384, 4096], P('scan', 'chan'), may hold values from -48 to 48
- chan_weight: bfloat16 [16384, 4096], P('scan', 'chan'), may hold values from 0.25 to 4
- kernel: bfloat16 [16384, 128], P('scan'), may hold values from 0.019897461 to 1
- tile_map: int32 [16384], P('scan'), may hold values from 0 to 63, as said below
- tile_slot: int32 [64], replicated, may hold values from 0 to 63, as said below
Outputs:
- baseline_coef: float32 [5, 8192], P(None, ('scan', 'chan'))
- residual: float32 [8192, 4096], P(('scan', 'chan'))
The draws below stay inside these ranges and needn't reach their ends.
Inputs may be any that keep to these rules, and one draw needn't show every extreme that they name: `tile_map`: each spectrum names one of the 64 tiles; among the spectra of one index of scan at most 128 name tiles of any one owner, and one owner receives exactly 128 from every index of scan. `tile_slot`: every position occurs once; the tiles at positions r * 4 to (r + 1) * 4 - 1 belong to index r of scan.
All inputs are finite; a program needn't handle non-finite values.
Results may differ from the reference program's by a relative error of at most 0.0026.
Values may be sent and summed in bfloat16 or wider, within the bound.
No kernel may reach another device: no remote copies, remote signals or barrier semaphores. Data moves between devices by JAX's collectives and lax.ppermute only.
A program may use at most 64 MiB of HBM per device.

```python
import math
import jax
import jax.numpy as jnp
from jax import lax

CHANNELS = 4096
PIX_TILE = 128
BASIS = 5
TILE_DEV = 4
SPEC_DEV = 1024
NTILES = 64
SPECTRA = 16384
NPIX = 8192
N_SCAN = 16


def owner_tables(key):
    slot_key, owner_key, count_key, sub_key = jax.random.split(key, 4)
    tile_slot = jax.random.permutation(slot_key, NTILES).astype(jnp.int32)
    inverse = jnp.argsort(tile_slot).astype(jnp.int32)
    full_owner = jax.random.randint(owner_key, (), 0, N_SCAN).astype(jnp.int32)
    capacity = 2 * SPEC_DEV // N_SCAN

    def block_owners(block_key):
        order_key, share_key, shuffle_key = jax.random.split(block_key, 3)
        order = jax.random.permutation(order_key, N_SCAN).astype(jnp.int32)
        order = jnp.where(order == full_owner, order[0], order)
        order = order.at[0].set(full_owner)
        small = jax.random.randint(share_key, (N_SCAN // 2,), capacity // 4, capacity // 2 + 1).astype(jnp.int32)
        small = small.at[0].set(0)
        paired = jnp.stack([capacity - small, small], axis=1).reshape(N_SCAN)
        counts = jnp.zeros((N_SCAN,), jnp.int32).at[order].set(paired)
        bounds = jnp.cumsum(counts)
        rows = jnp.arange(SPEC_DEV, dtype=jnp.int32)
        owner_sorted = jnp.sum((rows[:, None] >= bounds[None, :]).astype(jnp.int32), axis=1)
        shuffle = jax.random.permutation(shuffle_key, SPEC_DEV)
        return owner_sorted[shuffle].astype(jnp.int32)
    owners = jax.vmap(block_owners)(jax.random.split(count_key, N_SCAN)).reshape(SPECTRA)
    within = jax.random.randint(sub_key, (SPECTRA,), 0, TILE_DEV).astype(jnp.int32)
    tile_map = inverse[owners * TILE_DEV + within]
    return (tile_slot, tile_map)


def draw_tile_slot(key, part):
    tables = owner_tables(key)
    return tables[0]


def draw_tile_map(key, part):
    tables = owner_tables(key)
    return tables[1]


def draw_spectra(key, part):
    key = jax.random.fold_in(key, 11)
    common_key, own_key, phase_key, noise_key = jax.random.split(key, 4)
    channel = jnp.arange(CHANNELS).astype(jnp.float32)
    abscissa = (2.0 * channel + 1.0) / CHANNELS - 1.0
    common = 3.0 * jax.random.normal(common_key, (4,), jnp.float32)
    own = 1.5 * jax.random.normal(own_key, (SPECTRA, 4), jnp.float32)
    smooth = jnp.zeros((SPECTRA, CHANNELS), jnp.float32)
    for degree in range(4):
        smooth = smooth + (common[degree] + own[:, degree])[:, None] * (abscissa ** degree)[None, :]
    phase = jax.random.uniform(phase_key, (), jnp.float32, -3.14159, 3.14159)
    wave = 2.0 * jnp.sin(6.2831853 * 3.0 * channel / CHANNELS + phase)
    noise = jnp.clip(4.0 * jax.random.normal(noise_key, (SPECTRA, CHANNELS), jnp.float32), -16.0, 16.0)
    total = jnp.clip(smooth + wave[None, :] + noise, -48.0, 48.0)
    return total.astype(jnp.bfloat16)


def level_of(key, shape, cuts, low, largest):
    def one(axis_at, shards_of):
        heights = jax.random.uniform(jax.random.fold_in(jax.random.fold_in(key, 6), axis_at), (shards_of,), jnp.float32, low / len(cuts), largest / len(cuts))
        return jnp.repeat(jnp.exp(heights), shape[axis_at] // shards_of).reshape((-1,) + (1,) * (len(shape) - axis_at - 1))

    factor_of = one(*cuts[0])
    for cut in cuts[1:]:
        factor_of = factor_of * one(*cut)
    return factor_of


def setup_inputs(seed: int = 0) -> dict:
    key_of = jax.random.split(jax.random.key(seed), 6)
    return {
        "spectra": draw_spectra(jax.random.fold_in(key_of[5], 71), 0),
        "chan_weight": jnp.clip(jnp.exp(math.log(4.0) - 2.7725887 * jax.random.uniform(key_of[1], (SPECTRA, CHANNELS), jnp.float32) ** level_of(key_of[1], (SPECTRA, CHANNELS), ((0, 16), (1, 16)), -0.2, 0.2)), 0.25, 4.0).astype(jnp.bfloat16),
        "kernel": jnp.clip(jnp.exp(math.log(1.0) - 3.9171631 * jax.random.uniform(key_of[2], (SPECTRA, PIX_TILE), jnp.float32) ** level_of(key_of[2], (SPECTRA, PIX_TILE), ((0, 16),), -0.2, 0.2)), 0.019897461, 1.0).astype(jnp.bfloat16),
        "tile_map": draw_tile_map(jax.random.fold_in(key_of[5], 71), 0),
        "tile_slot": draw_tile_slot(jax.random.fold_in(key_of[5], 71), 0),
    }


def basis_table(total, terms):
    abscissa = (2.0 * jnp.arange(total).astype(jnp.float32) + 1.0) / total - 1.0
    columns = []
    for degree in range(terms):
        column = abscissa ** degree
        for earlier in columns:
            column = column - jnp.sum(earlier * column) * earlier
        column = column / jnp.sqrt(jnp.sum(column * column))
        columns.append(column)
    return jnp.stack(columns, axis=1)

def reference(spectra, chan_weight, kernel, tile_map, tile_slot):
    slot_ids = tile_slot[tile_map].astype(jnp.int32)
    weighted = (chan_weight.astype(jnp.float32) * spectra.astype(jnp.float32)).astype(jnp.bfloat16)
    stacked = jnp.concatenate([weighted, chan_weight], axis=1).astype(jnp.float32)
    kernel_cols = kernel.T.astype(jnp.float32)

    def one_slot(target):
        masked = jnp.where(slot_ids[None, :] == target, kernel_cols, jnp.zeros((), kernel_cols.dtype))
        return jnp.dot(masked, stacked, precision=lax.Precision.HIGHEST)
    gridded = lax.map(one_slot, jnp.arange(NTILES, dtype=jnp.int32))
    grid_cube = (gridded[..., :CHANNELS] / (gridded[..., CHANNELS:] + 1.0)).reshape(NPIX, CHANNELS)
    basis = basis_table(CHANNELS, BASIS)
    coeffs = jnp.einsum('ck,pc->kp', basis, grid_cube, precision=lax.Precision.HIGHEST)
    residual = grid_cube - jnp.einsum('ck,kp->pc', basis, coeffs, precision=lax.Precision.HIGHEST)
    return (coeffs, residual)
```

```python
import functools

import jax
import jax.numpy as jnp
import numpy as np
from jax import lax
from jax.experimental import pallas as pl
from jax.experimental.pallas import tpu as pltpu
from jax.sharding import PartitionSpec as P

CHANNELS = 4096
BASIS = 5
CAP = 128
TILES = 4
LANES = 128
HIGHEST = lax.Precision.HIGHEST


def orthonormal(abscissa, terms):
    columns = []
    for degree in range(terms):
        column = abscissa**degree
        for earlier in columns:
            column = column - np.sum(earlier * column) * earlier
        columns.append(column / np.sqrt(np.sum(column * column)))
    return np.stack(columns, axis=1)


def tables(channels, parts):
    width = channels // parts
    basis = orthonormal((2.0 * np.arange(channels) + 1.0) / channels - 1.0, BASIS)
    local = orthonormal((2.0 * np.arange(width) + 1.0) / width - 1.0, BASIS)
    mix = np.stack([local.T @ basis[c * width : (c + 1) * width] for c in range(parts)])
    project = np.zeros((width, LANES))
    for copy in range(3):
        project[:, copy * BASIS : (copy + 1) * BASIS] = local
    expand = np.zeros((LANES, width))
    expand[:BASIS] = local.T
    combine = np.zeros((parts * 8 + 8, parts * 16))
    for c in range(parts):
        for copy in range(3):
            at = c * 16 + copy * BASIS
            combine[parts * 8 : parts * 8 + BASIS, at : at + BASIS] = mix[c].T
            combine[c * 8 : c * 8 + BASIS, at : at + BASIS] += np.eye(BASIS)
    for c in range(parts):
        combine[c * 8 : c * 8 + BASIS] -= mix[c] @ combine[parts * 8 : parts * 8 + BASIS]
    short = np.zeros((8, width))
    short[:BASIS] = local.T
    return [a.astype(np.float32) for a in (project, expand, combine, short)]


def pack_kernel(owners, step_owners, slot_ref, map_ref, spec_ref, cw_ref, ker_ref, out_ref, rows, dest):
    step = pl.program_id(0)
    groups = map_ref.shape[0]
    count = groups * LANES
    width = spec_ref.shape[1]

    @pl.when(step == 0)
    def _():
        tile_map = map_ref[...]
        slot = jnp.zeros_like(tile_map)
        for t in range(owners * TILES):
            slot = jnp.where(tile_map == t, slot_ref[t], slot)
        owner = slot // TILES
        masks = jnp.concatenate(
            [(owner == o).astype(jnp.float32) for o in range(owners)], axis=0
        ).astype(jnp.bfloat16)
        size = owners * groups
        at0 = lax.broadcasted_iota(jnp.int32, (LANES, LANES), 0)
        at1 = lax.broadcasted_iota(jnp.int32, (LANES, LANES), 1)
        earlier = (at0 < at1).astype(jnp.float32).astype(jnp.bfloat16)
        ones = jnp.ones((LANES, LANES), jnp.bfloat16)
        r0 = lax.broadcasted_iota(jnp.int32, (size, size), 0)
        r1 = lax.broadcasted_iota(jnp.int32, (size, size), 1)
        above = jnp.logical_and(r0 // groups == r1 // groups, r1 < r0)
        above = above.astype(jnp.float32).astype(jnp.bfloat16)
        total = jnp.dot(masks, ones, preferred_element_type=jnp.float32).astype(jnp.bfloat16)
        rank = jnp.dot(masks, earlier, preferred_element_type=jnp.float32)
        rank = rank + jnp.dot(above, total, preferred_element_type=jnp.float32)
        place = jnp.zeros(owner.shape, jnp.float32)
        for o in range(owners):
            place = jnp.where(
                owner == o, rank[o * groups : (o + 1) * groups] + float(o * CAP), place
            )
        dest[...] = place.astype(jnp.int32)
        tile = (slot - owner * TILES + 1).astype(jnp.float32)
        turned = jnp.concatenate([tile] * (LANES // groups), axis=0).T
        for r in range(groups):
            column = jnp.broadcast_to(turned[:, r : r + 1], (LANES, LANES))
            rows[r * LANES : (r + 1) * LANES, 2 * width + LANES :] = column.astype(jnp.bfloat16)
        cw = cw_ref[...]
        weighted = cw.astype(jnp.float32) * spec_ref[...].astype(jnp.float32)
        rows[:, :width] = weighted.astype(jnp.bfloat16)
        rows[:, width : 2 * width] = cw
        rows[:, 2 * width : 2 * width + LANES] = ker_ref[...]

    amount = step_owners * CAP
    wanted = lax.broadcasted_iota(jnp.int32, (amount, LANES), 0) + step * amount
    chosen = jnp.concatenate(
        [
            (wanted == dest[r : r + 1, :]).astype(jnp.float32).astype(jnp.bfloat16)
            for r in range(groups)
        ],
        axis=1,
    )
    for half in range(2):
        got = jnp.dot(
            chosen, rows[:, half * width : (half + 1) * width], preferred_element_type=jnp.float32
        ).astype(jnp.bfloat16)
        for o in range(step_owners):
            for b in range(width // LANES):
                at = (half * (width // LANES) + b) * CAP
                out_ref[o, at : at + CAP, :] = got[
                    o * CAP : (o + 1) * CAP, b * LANES : (b + 1) * LANES
                ]
    got = jnp.dot(chosen, rows[:, 2 * width :], preferred_element_type=jnp.float32)
    at = 2 * width // LANES * CAP
    for o in range(step_owners):
        part = got[o * CAP : (o + 1) * CAP]
        out_ref[o, at : at + LANES, :] = part[:, :LANES].T.astype(jnp.bfloat16)
        out_ref[o, at + LANES : at + LANES + 16, :] = part[:, LANES:].T[:16].astype(jnp.bfloat16)


def grid_kernel(width, in_ref, project_ref, expand_ref, out_ref, total):
    step = pl.program_id(0)
    senders = in_ref.shape[0]
    blocks = 2 * width // LANES
    spectra = jnp.concatenate(
        [
            jnp.concatenate([in_ref[s, b * CAP : (b + 1) * CAP, :] for b in range(blocks)], axis=1)
            for s in range(senders)
        ],
        axis=0,
    )
    at = blocks * CAP
    columns = []
    for s in range(senders):
        kernel_cols = in_ref[s, at : at + LANES, :]
        tile = in_ref[s, at + LANES : at + LANES + 16, :].astype(jnp.float32)
        pieces = []
        for t in range(TILES):
            here = (tile == float(t + 1)).astype(jnp.float32).astype(jnp.bfloat16)
            pieces.append(kernel_cols * jnp.concatenate([here] * (LANES // 16), axis=0))
        columns.append(jnp.concatenate(pieces, axis=0))
    masked = jnp.concatenate(columns, axis=1)
    product = jnp.dot(masked, spectra, preferred_element_type=jnp.float32)

    @pl.when(step == 0)
    def _():
        total[...] = product

    @pl.when(step > 0)
    def _():
        total[...] += product

    @pl.when(step == pl.num_programs(0) - 1)
    def _():
        cube = total[:, :width] / (total[:, width:] + 1.0)
        coef = jnp.dot(cube, project_ref[...], precision=HIGHEST, preferred_element_type=jnp.float32)
        rest = cube - jnp.dot(
            coef, expand_ref[...], precision=HIGHEST, preferred_element_type=jnp.float32
        )
        rest = rest.astype(jnp.bfloat16)
        parts = out_ref.shape[0]
        mine = rest.shape[0] // parts
        turned = coef.T[:16]
        high = turned.astype(jnp.bfloat16).astype(jnp.float32)
        left = turned - high
        middle = left.astype(jnp.bfloat16).astype(jnp.float32)
        low = left - middle
        row = lax.broadcasted_iota(jnp.int32, turned.shape, 0)
        sent = jnp.where(row < BASIS, high, jnp.where(row < 2 * BASIS, middle, low))
        sent = jnp.where(row < 3 * BASIS, sent, 0.0)
        for c in range(parts):
            at = c * mine
            for b in range(width // LANES):
                out_ref[c, b * mine : (b + 1) * mine, :] = rest[
                    at : at + mine, b * LANES : (b + 1) * LANES
                ]
            group = sent[:, at // LANES * LANES : at // LANES * LANES + LANES]
            if at % LANES:
                group = pltpu.roll(group, LANES - at % LANES, axis=1)
            last = width // LANES * mine
            out_ref[c, last : last + 16, :] = group.astype(jnp.bfloat16)


def final_kernel(width, in_ref, combine_ref, short_ref, coef_ref, res_ref):
    parts = in_ref.shape[0]
    mine = res_ref.shape[0]
    last = width // LANES * mine
    sent = jnp.concatenate(
        [in_ref[c, last : last + 16, :].astype(jnp.float32) for c in range(parts)], axis=0
    )
    mixed = jnp.dot(combine_ref[...], sent, precision=HIGHEST, preferred_element_type=jnp.float32)
    coef_ref[...] = mixed[parts * 8 : parts * 8 + BASIS, :mine]
    turned = mixed[: parts * 8].T[:mine]
    for c in range(parts):
        rest = jnp.concatenate(
            [in_ref[c, b * mine : (b + 1) * mine, :] for b in range(width // LANES)], axis=1
        ).astype(jnp.float32)
        for k in range(BASIS):
            rest = rest + turned[:, c * 8 + k : c * 8 + k + 1] * short_ref[k : k + 1, :]
        res_ref[:, c * width : (c + 1) * width] = rest


def per_device(owners, parts, spectra, chan_weight, kernel, tile_map, tile_slot):
    count, width = spectra.shape
    pixels = TILES * LANES
    mine = pixels // parts
    project, expand, combine, short = (jnp.asarray(a) for a in tables(CHANNELS, parts))
    limit = pltpu.CompilerParams(vmem_limit_bytes=40 * 2**20)
    whole = lambda shape: pl.BlockSpec(shape, lambda i: (0,) * len(shape))

    long = 2 * width // LANES * CAP + LANES + 16
    at_once = 4
    packed = pl.pallas_call(
        functools.partial(pack_kernel, owners, at_once),
        grid=(owners // at_once,),
        out_shape=jax.ShapeDtypeStruct((owners, long, LANES), jnp.bfloat16),
        in_specs=[
            pl.BlockSpec(memory_space=pltpu.SMEM),
            whole((count // LANES, LANES)),
            whole((count, width)),
            whole((count, width)),
            whole((count, LANES)),
        ],
        out_specs=pl.BlockSpec((at_once, long, LANES), lambda i: (i, 0, 0)),
        scratch_shapes=[
            pltpu.VMEM((count, 2 * width + 2 * LANES), jnp.bfloat16),
            pltpu.VMEM((count // LANES, LANES), jnp.int32),
        ],
        compiler_params=limit,
    )(tile_slot, tile_map.reshape(count // LANES, LANES), spectra, chan_weight, kernel)

    routed = lax.all_to_all(packed, "scan", split_axis=0, concat_axis=0, tiled=True)

    tall = width // LANES * mine + 16
    gridded = pl.pallas_call(
        functools.partial(grid_kernel, width),
        grid=(owners // at_once,),
        out_shape=jax.ShapeDtypeStruct((parts, tall, LANES), jnp.bfloat16),
        in_specs=[
            pl.BlockSpec((at_once, long, LANES), lambda i: (i, 0, 0)),
            whole(project.shape),
            whole(expand.shape),
        ],
        out_specs=whole((parts, tall, LANES)),
        scratch_shapes=[pltpu.VMEM((pixels, 2 * width), jnp.float32)],
        compiler_params=limit,
    )(routed, project, expand)

    rows = lax.all_to_all(gridded, "chan", split_axis=0, concat_axis=0, tiled=True)

    return pl.pallas_call(
        functools.partial(final_kernel, width),
        out_shape=[
            jax.ShapeDtypeStruct((BASIS, mine), jnp.float32),
            jax.ShapeDtypeStruct((mine, CHANNELS), jnp.float32),
        ],
        compiler_params=limit,
    )(rows, combine, short)


def solution(mesh):
    placed = (P("scan", "chan"), P("scan", "chan"), P("scan", None), P("scan"), P())
    return jax.shard_map(
        functools.partial(per_device, mesh.shape["scan"], mesh.shape["chan"]),
        mesh=mesh,
        in_specs=placed,
        out_specs=(P(None, ("scan", "chan")), P(("scan", "chan"), None)),
        check_vma=False,
    )
```

```python
import functools

import jax
import jax.numpy as jnp
import numpy as np
from jax import lax
from jax.experimental import pallas as pl
from jax.experimental.pallas import tpu as pltpu
from jax.sharding import PartitionSpec as P

CHANNELS = 4096
BASIS = 5
CAP = 128
TILES = 4
LANES = 128


def orthonormal(abscissa, terms):
    columns = []
    for degree in range(terms):
        column = abscissa**degree
        for earlier in columns:
            column = column - np.sum(earlier * column) * earlier
        columns.append(column / np.sqrt(np.sum(column * column)))
    return np.stack(columns, axis=1)


def split_terms(values, terms):
    left = np.asarray(values, np.float64)
    parts = []
    for _ in range(terms):
        part = left.astype(jnp.bfloat16)
        parts.append(part)
        left = left - part.astype(np.float64)
    return parts


LEFT = (0, 1, 2, 0, 0, 1)
RIGHT = (0, 0, 0, 1, 2, 1)


def tables(channels, parts):
    width = channels // parts
    basis = orthonormal((2.0 * np.arange(channels) + 1.0) / channels - 1.0, BASIS)
    local = orthonormal((2.0 * np.arange(width) + 1.0) / width - 1.0, BASIS)
    mix = np.stack([local.T @ basis[c * width : (c + 1) * width] for c in range(parts)])
    project = np.zeros((width, LANES))
    expand = np.zeros((LANES, width), jnp.bfloat16)
    terms = split_terms(local.T, 3)
    for group, term in enumerate(RIGHT):
        project[:, group * BASIS : (group + 1) * BASIS] = local
        expand[group * BASIS : (group + 1) * BASIS] = terms[term]
    project = np.concatenate(split_terms(project, 2), axis=1)
    combine = np.zeros((parts * 8 + 16, parts * 16))
    for c in range(parts):
        for copy in range(3):
            at = c * 16 + copy * BASIS
            combine[parts * 8 : parts * 8 + BASIS, at : at + BASIS] = mix[c].T
            combine[c * 8 : c * 8 + BASIS, at : at + BASIS] += np.eye(BASIS)
    for c in range(parts):
        combine[c * 8 : c * 8 + BASIS] -= mix[c] @ combine[parts * 8 : parts * 8 + BASIS]
    combine = np.concatenate(split_terms(combine, 3))
    short = np.zeros((parts, 8, width))
    short[:, :BASIS] = local.T
    short = split_terms(short.reshape(parts * 8, width), 2)
    short = np.concatenate([short[0], short[0], short[1]])
    return project, expand, combine, short


def dot(a, b):
    return jnp.dot(a, b, preferred_element_type=jnp.float32)


def one_hot(mask):
    return mask.astype(jnp.float32).astype(jnp.bfloat16)


def pack_kernel(
    owners, slot_hbm, map_hbm, spec_hbm, cw_hbm, ker_hbm, out_ref, slot_ref, map_ref, spec_ref, rows, sems
):
    groups = map_ref.shape[0]
    width = spec_ref.shape[1]
    copies = [
        pltpu.make_async_copy(slot_hbm, slot_ref, sems.at[0]),
        pltpu.make_async_copy(map_hbm, map_ref, sems.at[1]),
        pltpu.make_async_copy(spec_hbm, spec_ref, sems.at[2]),
        pltpu.make_async_copy(cw_hbm, rows.at[:, width : 2 * width], sems.at[3]),
        pltpu.make_async_copy(ker_hbm, rows.at[:, 2 * width : 2 * width + LANES], sems.at[4]),
    ]
    for copy in copies:
        copy.start()
    size = owners * groups
    at0 = lax.broadcasted_iota(jnp.int32, (LANES, LANES), 0)
    at1 = lax.broadcasted_iota(jnp.int32, (LANES, LANES), 1)
    earlier = one_hot(at0 < at1)
    ones = jnp.ones((LANES, LANES), jnp.bfloat16)
    r0 = lax.broadcasted_iota(jnp.int32, (size, size), 0)
    r1 = lax.broadcasted_iota(jnp.int32, (size, size), 1)
    above = one_hot(jnp.logical_and(r0 // groups == r1 // groups, r1 < r0))
    copies[0].wait()
    copies[1].wait()

    tile_map = map_ref[...]
    slot = jnp.zeros_like(tile_map)
    for t in range(owners * TILES):
        slot = jnp.where(tile_map == t, slot_ref[t], slot)
    owner = slot // TILES
    masks = jnp.concatenate(
        [(owner == o).astype(jnp.float32) for o in range(owners)], axis=0
    ).astype(jnp.bfloat16)
    total = dot(masks, ones).astype(jnp.bfloat16)
    rank = dot(masks, earlier) + dot(above, total)
    place = jnp.zeros(owner.shape, jnp.float32)
    for o in range(owners):
        place = jnp.where(owner == o, rank[o * groups : (o + 1) * groups] + float(o * CAP), place)
    place = place.astype(jnp.int32)
    tile = (slot - owner * TILES + 1).astype(jnp.float32)
    turned = jnp.concatenate([tile] * (LANES // groups), axis=0).T
    for r in range(groups):
        column = jnp.broadcast_to(turned[:, r : r + 1], (LANES, LANES))
        rows[r * LANES : (r + 1) * LANES, 2 * width + LANES :] = column.astype(jnp.bfloat16)

    at_once = 2
    amount = at_once * CAP
    at = 2 * width // LANES * CAP
    for step in range(owners // at_once):
        wanted = lax.broadcasted_iota(jnp.int32, (amount, LANES), 0) + step * amount
        chosen = jnp.concatenate(
            [one_hot(wanted == place[r : r + 1, :]) for r in range(groups)], axis=1
        )
        if step == 0:
            copies[2].wait()
            copies[3].wait()
            weighted = rows[:, width : 2 * width].astype(jnp.float32) * spec_ref[...].astype(jnp.float32)
            rows[:, :width] = weighted.astype(jnp.bfloat16)
            copies[4].wait()
        for half in range(2):
            got = dot(chosen, rows[:, half * width : (half + 1) * width]).astype(jnp.bfloat16)
            for o in range(at_once):
                for b in range(width // LANES):
                    to = (half * (width // LANES) + b) * CAP
                    out_ref[step * at_once + o, to : to + CAP, :] = got[
                        o * CAP : (o + 1) * CAP, b * LANES : (b + 1) * LANES
                    ]
        got = dot(chosen, rows[:, 2 * width :])
        for o in range(at_once):
            part = got[o * CAP : (o + 1) * CAP]
            to = step * at_once + o
            out_ref[to, at : at + LANES, :] = part[:, :LANES].T.astype(jnp.bfloat16)
            out_ref[to, at + LANES : at + LANES + 16, :] = part[:, LANES:].T[:16].astype(jnp.bfloat16)


def grid_kernel(width, in_ref, project_ref, expand_ref, out_ref):
    senders = in_ref.shape[0]
    blocks = 2 * width // LANES
    at_once = 4
    at = blocks * CAP
    parts = out_ref.shape[0]
    mine = TILES * LANES // parts
    last = width // LANES * mine
    total = None
    for first in range(0, senders, at_once):
        group = range(first, first + at_once)
        spectra = jnp.concatenate(
            [
                jnp.concatenate(
                    [in_ref[s, b * CAP : (b + 1) * CAP, :] for b in range(blocks)], axis=1
                )
                for s in group
            ],
            axis=0,
        )
        columns = []
        for s in group:
            kernel_cols = in_ref[s, at : at + LANES, :]
            tile = in_ref[s, at + LANES : at + LANES + 16, :].astype(jnp.float32)
            pieces = []
            for t in range(TILES):
                here = one_hot(tile == float(t + 1))
                pieces.append(kernel_cols * jnp.concatenate([here] * (LANES // 16), axis=0))
            columns.append(jnp.concatenate(pieces, axis=0))
        product = dot(jnp.concatenate(columns, axis=1), spectra)
        total = product if total is None else total + product

    cube = total[:, :width] / (total[:, width:] + 1.0)
    high = cube.astype(jnp.bfloat16)
    low = (cube - high.astype(jnp.float32)).astype(jnp.bfloat16)
    both = dot(high, project_ref[...])
    coef = both[:, :LANES] + (both[:, LANES:] + dot(low, project_ref[:, :LANES]))
    first = coef.astype(jnp.bfloat16).astype(jnp.float32)
    left = coef - first
    second = left.astype(jnp.bfloat16).astype(jnp.float32)
    third = left - second
    group = lax.broadcasted_iota(jnp.int32, coef.shape, 1) // BASIS
    terms = jnp.where(group == 2, third, first)
    terms = jnp.where(jnp.logical_or(group == 1, group == 5), second, terms)
    rest = (cube - dot(terms.astype(jnp.bfloat16), expand_ref[...])).astype(jnp.bfloat16)
    sent = terms.T[:16]
    pixels = TILES * LANES
    for at_pixel in range(0, pixels, mine):
        c = at_pixel // mine
        for b in range(width // LANES):
            out_ref[c, b * mine : (b + 1) * mine, :] = rest[
                at_pixel : at_pixel + mine, b * LANES : (b + 1) * LANES
            ]
        turned = sent[:, at_pixel // LANES * LANES : at_pixel // LANES * LANES + LANES]
        if at_pixel % LANES:
            turned = pltpu.roll(turned, LANES - at_pixel % LANES, axis=1)
        out_ref[c, last : last + 16, :] = turned.astype(jnp.bfloat16)


def final_kernel(width, in_ref, combine_ref, short_ref, coef_ref, res_ref):
    parts = in_ref.shape[0]
    mine = res_ref.shape[0]
    last = width // LANES * mine
    sent = jnp.concatenate([in_ref[c, last : last + 16, :] for c in range(parts)], axis=0)
    mixed = dot(combine_ref[...], sent)
    size = parts * 8 + 16
    mixed = mixed[:size] + (mixed[size : 2 * size] + mixed[2 * size :])
    coef_ref[...] = mixed[parts * 8 : parts * 8 + BASIS, :mine]
    turned = mixed[: parts * 8].T[:mine]
    high = turned.astype(jnp.bfloat16)
    low = (turned - high.astype(jnp.float32)).astype(jnp.bfloat16)
    both = jnp.concatenate([high, low, high], axis=1)
    owner = lax.broadcasted_iota(jnp.int32, both.shape, 1) % (parts * 8) // 8
    zero = jnp.zeros_like(both)
    spread = jnp.concatenate([jnp.where(owner == c, both, zero) for c in range(parts)], axis=0)
    added = dot(spread, short_ref[...])
    for c in range(parts):
        rest = jnp.concatenate(
            [in_ref[c, b * mine : (b + 1) * mine, :] for b in range(width // LANES)], axis=1
        ).astype(jnp.float32)
        res_ref[:, c * width : (c + 1) * width] = rest + added[c * mine : (c + 1) * mine]


def per_device(owners, parts, spectra, chan_weight, kernel, tile_map, tile_slot):
    count, width = spectra.shape
    mine = TILES * LANES // parts
    project, expand, combine, short = (jnp.asarray(a) for a in tables(CHANNELS, parts))
    limit = pltpu.CompilerParams(vmem_limit_bytes=40 * 2**20)
    hbm = pl.BlockSpec(memory_space=pltpu.HBM)

    long = 2 * width // LANES * CAP + LANES + 16
    packed = pl.pallas_call(
        functools.partial(pack_kernel, owners),
        out_shape=jax.ShapeDtypeStruct((owners, long, LANES), jnp.bfloat16),
        in_specs=[hbm] * 5,
        scratch_shapes=[
            pltpu.SMEM(tile_slot.shape, jnp.int32),
            pltpu.VMEM((count // LANES, LANES), jnp.int32),
            pltpu.VMEM((count, width), jnp.bfloat16),
            pltpu.VMEM((count, 2 * width + 2 * LANES), jnp.bfloat16),
            pltpu.SemaphoreType.DMA((5,)),
        ],
        compiler_params=limit,
    )(
        *[
            pltpu.with_memory_space_constraint(a, pltpu.HBM)
            for a in (
                tile_slot,
                tile_map.reshape(count // LANES, LANES),
                spectra,
                chan_weight,
                kernel,
            )
        ]
    )

    routed = lax.all_to_all(packed, "scan", split_axis=0, concat_axis=0, tiled=True)

    tall = width // LANES * mine + 16
    gridded = pl.pallas_call(
        functools.partial(grid_kernel, width),
        out_shape=jax.ShapeDtypeStruct((parts, tall, LANES), jnp.bfloat16),
        compiler_params=limit,
    )(routed, project, expand)

    rows = lax.all_to_all(gridded, "chan", split_axis=0, concat_axis=0, tiled=True)

    return pl.pallas_call(
        functools.partial(final_kernel, width),
        out_shape=[
            jax.ShapeDtypeStruct((BASIS, mine), jnp.float32),
            jax.ShapeDtypeStruct((mine, CHANNELS), jnp.float32),
        ],
        compiler_params=limit,
    )(rows, combine, short)


def solution(mesh):
    placed = (P("scan", "chan"), P("scan", "chan"), P("scan", None), P("scan"), P())
    return jax.shard_map(
        functools.partial(per_device, mesh.shape["scan"], mesh.shape["chan"]),
        mesh=mesh,
        in_specs=placed,
        out_specs=(P(None, ("scan", "chan")), P(("scan", "chan"), None)),
        check_vma=False,
    )
```

```python
import functools

import jax
import jax.numpy as jnp
import numpy as np
from jax import lax
from jax.experimental import pallas as pl
from jax.experimental.pallas import tpu as pltpu
from jax.sharding import PartitionSpec as P

CHANNELS = 4096
BASIS = 5
CAP = 128
TILES = 4
LANES = 128
ALIGN = 16
HALF = LANES // 2


def orthonormal(abscissa, terms):
    columns = []
    for degree in range(terms):
        column = abscissa**degree
        for earlier in columns:
            column = column - np.sum(earlier * column) * earlier
        columns.append(column / np.sqrt(np.sum(column * column)))
    return np.stack(columns, axis=1)


def split_terms(values, terms):
    left = np.asarray(values, np.float64)
    parts = []
    for _ in range(terms):
        part = left.astype(jnp.bfloat16)
        parts.append(part)
        left = left - part.astype(np.float64)
    return parts


LEFT = (0, 1, 2, 0, 0, 1)
RIGHT = (0, 0, 0, 1, 2, 1)


def tables(channels, parts):
    width = channels // parts
    basis = orthonormal((2.0 * np.arange(channels) + 1.0) / channels - 1.0, BASIS)
    local = orthonormal((2.0 * np.arange(width) + 1.0) / width - 1.0, BASIS)
    mix = np.stack([local.T @ basis[c * width : (c + 1) * width] for c in range(parts)])
    project = np.zeros((width, LANES))
    expand = np.zeros((LANES, width), jnp.bfloat16)
    terms = split_terms(local.T, 3)
    for group, term in enumerate(RIGHT):
        project[:, group * BASIS : (group + 1) * BASIS] = local
        expand[group * BASIS : (group + 1) * BASIS] = terms[term]
    project = np.concatenate(split_terms(project, 2), axis=1)
    combine = np.zeros((parts * 8 + 16, parts * 16))
    for c in range(parts):
        for copy in range(3):
            at = c * 16 + copy * BASIS
            combine[parts * 8 : parts * 8 + BASIS, at : at + BASIS] = mix[c].T
            combine[c * 8 : c * 8 + BASIS, at : at + BASIS] += np.eye(BASIS)
    for c in range(parts):
        combine[c * 8 : c * 8 + BASIS] -= mix[c] @ combine[parts * 8 : parts * 8 + BASIS]
    combine = np.concatenate(split_terms(combine, 3))
    short = np.zeros((parts, 8, width))
    short[:, :BASIS] = local.T
    short = split_terms(short.reshape(parts * 8, width), 2)
    short = np.concatenate([short[0], short[0], short[1]])
    return project, expand, combine, short


def dot(a, b):
    return jnp.dot(a, b, preferred_element_type=jnp.float32)


def one_hot(mask):
    return mask.astype(jnp.float32).astype(jnp.bfloat16)


def pack_kernel(
    owners,
    slot_hbm,
    map_hbm,
    spec_hbm,
    cw_hbm,
    ker_hbm,
    out_ref,
    slot_ref,
    map_ref,
    spec_ref,
    rows,
    ordered,
    bounds,
    limits,
    sems,
):
    core = lax.axis_index("chan") % 2
    groups = map_ref.shape[0]
    width = spec_ref.shape[1]
    copies = [
        pltpu.make_async_copy(slot_hbm, slot_ref, sems.at[0]),
        pltpu.make_async_copy(map_hbm, map_ref, sems.at[1]),
        pltpu.make_async_copy(cw_hbm, rows.at[:, width : 2 * width], sems.at[2]),
        pltpu.make_async_copy(ker_hbm, rows.at[:, 2 * width : 2 * width + LANES], sems.at[3]),
        pltpu.make_async_copy(spec_hbm, spec_ref, sems.at[4]),
    ]
    for copy in copies:
        copy.start()
    size = owners * groups
    at0 = lax.broadcasted_iota(jnp.int32, (LANES, LANES), 0)
    at1 = lax.broadcasted_iota(jnp.int32, (LANES, LANES), 1)
    earlier = one_hot(at0 < at1)
    ones = jnp.ones((LANES, LANES), jnp.bfloat16)
    r0 = lax.broadcasted_iota(jnp.int32, (size, size), 0)
    r1 = lax.broadcasted_iota(jnp.int32, (size, size), 1)
    same = r0 // groups == r1 // groups
    above = one_hot(jnp.logical_and(same, r1 < r0))
    before = one_hot(r1 // groups < r0 // groups)
    copies[0].wait()
    copies[1].wait()

    tile_map = map_ref[...]
    slot = jnp.zeros_like(tile_map)
    for t in range(owners * TILES):
        slot = jnp.where(tile_map == t, slot_ref[t], slot)
    owner = slot // TILES
    masks = jnp.concatenate(
        [(owner == o).astype(jnp.float32) for o in range(owners)], axis=0
    ).astype(jnp.bfloat16)
    here = dot(masks, ones).astype(jnp.bfloat16)
    rank = dot(masks, earlier) + dot(above, here)
    count = dot(one_hot(same), here)
    room = jnp.floor((count + (ALIGN - 1.0)) * (1.0 / ALIGN)) * (ALIGN / float(groups))
    begin = dot(before, room.astype(jnp.bfloat16))
    rank = rank + begin
    place = jnp.zeros(owner.shape, jnp.float32)
    for o in range(owners):
        place = jnp.where(owner == o, rank[o * groups : (o + 1) * groups], place)
    place = place.astype(jnp.int32)
    table = jnp.where(at0 == at1 * groups, begin, 0.0)
    table = table + jnp.where(at0 == (at1 - 64) * groups, count, 0.0)
    bounds[...] = jnp.broadcast_to(
        jnp.sum(table, axis=0, keepdims=True), bounds.shape
    ).astype(jnp.int32)
    fetch = pltpu.make_async_copy(bounds, limits, sems.at[5])
    fetch.start()
    tile = (slot - owner * TILES + 1).astype(jnp.float32)
    turned = jnp.concatenate([tile] * (LANES // groups), axis=0).T
    for r in range(groups):
        column = jnp.broadcast_to(turned[:, r : r + 1], (LANES, LANES))
        rows[r * LANES : (r + 1) * LANES, 2 * width + LANES :] = column.astype(jnp.bfloat16)

    total = ordered.shape[0] - CAP
    amount = 256
    ordered[total:, :] = jnp.zeros((CAP, ordered.shape[1]), jnp.bfloat16)
    for step in range(total // amount):
        wanted = lax.broadcasted_iota(jnp.int32, (amount, LANES), 0) + step * amount
        chosen = jnp.concatenate(
            [one_hot(wanted == place[r : r + 1, :]) for r in range(groups)], axis=1
        )
        if step == 0:
            copies[2].wait()
            copies[4].wait()
            weighted = rows[:, width : 2 * width].astype(jnp.float32)
            weighted = weighted * spec_ref[...].astype(jnp.float32)
            rows[:, :width] = weighted.astype(jnp.bfloat16)
            copies[3].wait()
        ordered[step * amount : (step + 1) * amount, :] = dot(chosen, rows[...]).astype(jnp.bfloat16)
    fetch.wait()
    at = 2 * width // LANES * CAP
    for o in range(owners):
        window = pl.ds(pl.multiple_of(limits[0, o], ALIGN), CAP)
        for b in range(2 * width // LANES):
            out_ref[o, b * CAP : (b + 1) * CAP, :] = ordered[window, b * LANES : (b + 1) * LANES]
        part = ordered[window, 2 * width :].astype(jnp.float32)
        turned = part[:, :LANES].T
        turned = jnp.where(core == 0, turned[:HALF], turned[HALF:])
        out_ref[o, at : at + HALF, :] = turned.astype(jnp.bfloat16)
        tiles = part[:, LANES:].T[:16]
        slots = lax.broadcasted_iota(jnp.int32, tiles.shape, 1)
        tiles = jnp.where(slots < limits[0, 64 + o], tiles, 0.0)
        out_ref[o, at + HALF : at + HALF + 16, :] = tiles.astype(jnp.bfloat16)


def grid_kernel(width, other, in_ref, cols_ref, project_ref, expand_ref, *refs):
    out_ref = refs[-1]
    half = (lax.axis_index("chan") + other) % 2
    senders = in_ref.shape[0]
    blocks = 2 * width // LANES
    at_once = 4
    at = blocks * CAP
    parts = out_ref.shape[0]
    mine = TILES * LANES // parts
    last = width // LANES * mine
    total = None
    for first in range(0, senders, at_once):
        group = range(first, first + at_once)
        spectra = jnp.concatenate(
            [
                jnp.concatenate(
                    [in_ref[s, b * CAP : (b + 1) * CAP, :] for b in range(blocks)], axis=1
                )
                for s in group
            ],
            axis=0,
        )
        columns = []
        for s in group:
            kernel_cols = cols_ref[s]
            tile = in_ref[s, at + HALF : at + HALF + 16, :].astype(jnp.float32)
            pieces = []
            for t in range(TILES):
                here = one_hot(tile == float(t + 1))
                pieces.append(kernel_cols * jnp.concatenate([here] * (HALF // 16), axis=0))
            columns.append(jnp.concatenate(pieces, axis=0))
        product = dot(jnp.concatenate(columns, axis=1), spectra)
        total = product if total is None else total + product

    cube = total[:, :width] / (total[:, width:] + 1.0)
    high = cube.astype(jnp.bfloat16)
    low = (cube - high.astype(jnp.float32)).astype(jnp.bfloat16)
    both = dot(high, project_ref[...])
    coef = both[:, :LANES] + (both[:, LANES:] + dot(low, project_ref[:, :LANES]))
    first = coef.astype(jnp.bfloat16).astype(jnp.float32)
    left = coef - first
    second = left.astype(jnp.bfloat16).astype(jnp.float32)
    third = left - second
    group = lax.broadcasted_iota(jnp.int32, coef.shape, 1) // BASIS
    terms = jnp.where(group == 2, third, first)
    terms = jnp.where(jnp.logical_or(group == 1, group == 5), second, terms)
    rest = (cube - dot(terms.astype(jnp.bfloat16), expand_ref[...])).astype(jnp.bfloat16)
    sent = terms.T[:16]
    for at_pixel in range(0, TILES * HALF, mine):
        c = at_pixel // HALF * (LANES // mine) + half * (HALF // mine) + at_pixel % HALF // mine
        for b in range(width // LANES):
            out_ref[c, b * mine : (b + 1) * mine, :] = rest[
                at_pixel : at_pixel + mine, b * LANES : (b + 1) * LANES
            ]
        turned = sent[:, at_pixel // LANES * LANES : at_pixel // LANES * LANES + LANES]
        if at_pixel % LANES:
            turned = pltpu.roll(turned, LANES - at_pixel % LANES, axis=1)
        out_ref[c, last : last + 16, :] = turned.astype(jnp.bfloat16)


def final_kernel(width, in_ref, combine_ref, short_ref, coef_ref, res_ref):
    parts = in_ref.shape[0]
    mine = res_ref.shape[0]
    last = width // LANES * mine
    sent = jnp.concatenate([in_ref[c, last : last + 16, :] for c in range(parts)], axis=0)
    mixed = dot(combine_ref[...], sent)
    size = parts * 8 + 16
    mixed = mixed[:size] + (mixed[size : 2 * size] + mixed[2 * size :])
    coef_ref[...] = mixed[parts * 8 : parts * 8 + BASIS, :mine]
    turned = mixed[: parts * 8].T[:mine]
    high = turned.astype(jnp.bfloat16)
    low = (turned - high.astype(jnp.float32)).astype(jnp.bfloat16)
    both = jnp.concatenate([high, low, high], axis=1)
    owner = lax.broadcasted_iota(jnp.int32, both.shape, 1) % (parts * 8) // 8
    zero = jnp.zeros_like(both)
    spread = jnp.concatenate([jnp.where(owner == c, both, zero) for c in range(parts)], axis=0)
    added = dot(spread, short_ref[...])
    for c in range(parts):
        rest = jnp.concatenate(
            [in_ref[c, b * mine : (b + 1) * mine, :] for b in range(width // LANES)], axis=1
        ).astype(jnp.float32)
        res_ref[:, c * width : (c + 1) * width] = rest + added[c * mine : (c + 1) * mine]


def per_device(owners, parts, spectra, chan_weight, kernel, tile_map, tile_slot):
    count, width = spectra.shape
    mine = TILES * LANES // parts
    project, expand, combine, short = (jnp.asarray(a) for a in tables(CHANNELS, parts))
    limit = pltpu.CompilerParams(vmem_limit_bytes=40 * 2**20)
    hbm = pl.BlockSpec(memory_space=pltpu.HBM)

    long = 2 * width // LANES * CAP + HALF + 16
    room = count + owners * ALIGN
    packed = pl.pallas_call(
        functools.partial(pack_kernel, owners),
        out_shape=jax.ShapeDtypeStruct((owners, long, LANES), jnp.bfloat16),
        in_specs=[hbm] * 5,
        scratch_shapes=[
            pltpu.SMEM(tile_slot.shape, jnp.int32),
            pltpu.VMEM((count // LANES, LANES), jnp.int32),
            pltpu.VMEM((count, width), jnp.bfloat16),
            pltpu.VMEM((count, 2 * width + 2 * LANES), jnp.bfloat16),
            pltpu.VMEM((room + CAP, 2 * width + 2 * LANES), jnp.bfloat16),
            pltpu.VMEM((8, LANES), jnp.int32),
            pltpu.SMEM((8, LANES), jnp.int32),
            pltpu.SemaphoreType.DMA((6,)),
        ],
        compiler_params=limit,
    )(
        *[
            pltpu.with_memory_space_constraint(a, pltpu.HBM)
            for a in (
                tile_slot,
                tile_map.reshape(count // LANES, LANES),
                spectra,
                chan_weight,
                kernel,
            )
        ]
    )

    routed = lax.all_to_all(packed, "scan", split_axis=0, concat_axis=0, tiled=True)

    tall = width // LANES * mine + 16
    at = 2 * width // LANES * CAP
    mine_cols = routed[:, at : at + HALF, :]
    other_cols = lax.ppermute(mine_cols, "chan", [(c, c ^ 1) for c in range(parts)])
    whole = jax.ShapeDtypeStruct((parts, tall, LANES), jnp.bfloat16)
    vmem = pl.BlockSpec(memory_space=pltpu.VMEM)
    first = pl.pallas_call(
        functools.partial(grid_kernel, width, 0),
        out_shape=whole,
        in_specs=[vmem] * 4,
        out_specs=vmem,
        compiler_params=limit,
        cost_estimate=pl.CostEstimate(flops=10**9, bytes_accessed=3 * 10**6, transcendentals=0),
    )(routed, mine_cols, project, expand)
    gridded = pl.pallas_call(
        functools.partial(grid_kernel, width, 1),
        out_shape=whole,
        in_specs=[vmem] * 5,
        out_specs=vmem,
        input_output_aliases={4: 0},
        compiler_params=limit,
        cost_estimate=pl.CostEstimate(flops=10**9, bytes_accessed=3 * 10**6, transcendentals=0),
    )(routed, other_cols, project, expand, first)

    rows = lax.all_to_all(gridded, "chan", split_axis=0, concat_axis=0, tiled=True)

    return pl.pallas_call(
        functools.partial(final_kernel, width),
        out_shape=[
            jax.ShapeDtypeStruct((BASIS, mine), jnp.float32),
            jax.ShapeDtypeStruct((mine, CHANNELS), jnp.float32),
        ],
        compiler_params=limit,
    )(rows, combine, short)


def solution(mesh):
    placed = (P("scan", "chan"), P("scan", "chan"), P("scan", None), P("scan"), P())
    return jax.shard_map(
        functools.partial(per_device, mesh.shape["scan"], mesh.shape["chan"]),
        mesh=mesh,
        in_specs=placed,
        out_specs=(P(None, ("scan", "chan")), P(("scan", "chan"), None)),
        check_vma=False,
    )
```

```python
import functools

import jax
import jax.numpy as jnp
import numpy as np
from jax import lax
from jax.experimental import pallas as pl
from jax.experimental.pallas import tpu as pltpu
from jax.sharding import PartitionSpec as P

CHANNELS = 4096
BASIS = 5
CAP = 128
TILES = 4
LANES = 128
ALIGN = 16
HALF = LANES // 2


def orthonormal(abscissa, terms):
    columns = []
    for degree in range(terms):
        column = abscissa**degree
        for earlier in columns:
            column = column - np.sum(earlier * column) * earlier
        columns.append(column / np.sqrt(np.sum(column * column)))
    return np.stack(columns, axis=1)


def split_terms(values, terms):
    left = np.asarray(values, np.float64)
    parts = []
    for _ in range(terms):
        part = left.astype(jnp.bfloat16)
        parts.append(part)
        left = left - part.astype(np.float64)
    return parts


LEFT = (0, 1, 2, 0, 0, 1)
RIGHT = (0, 0, 0, 1, 2, 1)


def tables(channels, parts):
    width = channels // parts
    basis = orthonormal((2.0 * np.arange(channels) + 1.0) / channels - 1.0, BASIS)
    local = orthonormal((2.0 * np.arange(width) + 1.0) / width - 1.0, BASIS)
    mix = np.stack([local.T @ basis[c * width : (c + 1) * width] for c in range(parts)])
    project = np.zeros((width, LANES))
    expand = np.zeros((LANES, width), jnp.bfloat16)
    terms = split_terms(local.T, 3)
    for group, term in enumerate(RIGHT):
        project[:, group * BASIS : (group + 1) * BASIS] = local
        expand[group * BASIS : (group + 1) * BASIS] = terms[term]
    project = np.concatenate(split_terms(project, 2), axis=1)
    combine = np.zeros((parts * 8 + 16, parts * 16))
    for c in range(parts):
        for copy in range(3):
            at = c * 16 + copy * BASIS
            combine[parts * 8 : parts * 8 + BASIS, at : at + BASIS] = mix[c].T
            combine[c * 8 : c * 8 + BASIS, at : at + BASIS] += np.eye(BASIS)
    for c in range(parts):
        combine[c * 8 : c * 8 + BASIS] -= mix[c] @ combine[parts * 8 : parts * 8 + BASIS]
    combine = combine.reshape(-1, parts, 2, 8).transpose(0, 2, 1, 3).reshape(-1, parts * 16)
    combine = np.concatenate(split_terms(combine, 3))
    short = np.zeros((parts, 8, width))
    short[:, :BASIS] = local.T
    short = split_terms(short.reshape(parts * 8, width), 2)
    short = np.concatenate([short[0], short[0], short[1]])
    return project, expand, combine, short


def dot(a, b):
    return jnp.dot(a, b, preferred_element_type=jnp.float32)


def one_hot(mask):
    return mask.astype(jnp.float32).astype(jnp.bfloat16)


def pack_kernel(
    owners,
    slot_hbm,
    map_hbm,
    spec_hbm,
    cw_hbm,
    ker_hbm,
    out_ref,
    slot_ref,
    map_ref,
    rows,
    ordered,
    bounds,
    limits,
    sems,
):
    core = lax.axis_index("chan") % 2
    groups = map_ref.shape[0]
    width = spec_hbm.shape[1]
    copies = [
        pltpu.make_async_copy(slot_hbm, slot_ref, sems.at[0]),
        pltpu.make_async_copy(map_hbm, map_ref, sems.at[1]),
        pltpu.make_async_copy(cw_hbm, rows.at[:, width : 2 * width], sems.at[2]),
        pltpu.make_async_copy(ker_hbm, rows.at[:, 2 * width : 2 * width + LANES], sems.at[3]),
        pltpu.make_async_copy(spec_hbm, rows.at[:, :width], sems.at[4]),
    ]
    for copy in copies:
        copy.start()
    size = owners * groups
    at0 = lax.broadcasted_iota(jnp.int32, (LANES, LANES), 0)
    at1 = lax.broadcasted_iota(jnp.int32, (LANES, LANES), 1)
    earlier = one_hot(at0 < at1)
    ones = jnp.ones((LANES, LANES), jnp.bfloat16)
    r0 = lax.broadcasted_iota(jnp.int32, (size, size), 0)
    r1 = lax.broadcasted_iota(jnp.int32, (size, size), 1)
    same = r0 // groups == r1 // groups
    above = one_hot(jnp.logical_and(same, r1 < r0))
    before = one_hot(r1 // groups < r0 // groups)
    copies[0].wait()
    copies[1].wait()

    tile_map = map_ref[...]
    slot = jnp.zeros_like(tile_map)
    for t in range(owners * TILES):
        slot = jnp.where(tile_map == t, slot_ref[t], slot)
    owner = slot // TILES
    masks = jnp.concatenate(
        [(owner == o).astype(jnp.float32) for o in range(owners)], axis=0
    ).astype(jnp.bfloat16)
    here = dot(masks, ones).astype(jnp.bfloat16)
    rank = dot(masks, earlier) + dot(above, here)
    count = dot(one_hot(same), here)
    room = jnp.floor((count + (ALIGN - 1.0)) * (1.0 / ALIGN)) * (ALIGN / float(groups))
    begin = dot(before, room.astype(jnp.bfloat16))
    rank = rank + begin
    place = jnp.zeros(owner.shape, jnp.float32)
    for o in range(owners):
        place = jnp.where(owner == o, rank[o * groups : (o + 1) * groups], place)
    place = place.astype(jnp.int32)
    table = jnp.where(at0 == at1 * groups, begin, 0.0)
    table = table + jnp.where(at0 == (at1 - 64) * groups, count, 0.0)
    bounds[...] = jnp.broadcast_to(
        jnp.sum(table, axis=0, keepdims=True), bounds.shape
    ).astype(jnp.int32)
    fetch = pltpu.make_async_copy(bounds, limits, sems.at[5])
    fetch.start()
    tile = (slot - owner * TILES + 1).astype(jnp.float32)
    turned = jnp.concatenate([tile] * (LANES // groups), axis=0).T
    for r in range(groups):
        column = jnp.broadcast_to(turned[:, r : r + 1], (LANES, LANES))
        rows[r * LANES : (r + 1) * LANES, 2 * width + LANES :] = column.astype(jnp.bfloat16)

    total = ordered.shape[0] - CAP
    amount = 256
    ordered[total:, :] = jnp.zeros((CAP, ordered.shape[1]), jnp.bfloat16)
    for step in range(total // amount):
        wanted = lax.broadcasted_iota(jnp.int32, (amount, LANES), 0) + step * amount
        chosen = jnp.concatenate(
            [one_hot(wanted == place[r : r + 1, :]) for r in range(groups)], axis=1
        )
        if step == 0:
            for copy in copies[2:]:
                copy.wait()
        got = dot(chosen, rows[...])
        at = slice(step * amount, (step + 1) * amount)
        ordered[at, :width] = (got[:, :width] * got[:, width : 2 * width]).astype(jnp.bfloat16)
        ordered[at, width:] = got[:, width:].astype(jnp.bfloat16)
    fetch.wait()
    at = 2 * width // LANES * CAP
    for o in range(owners):
        window = pl.ds(pl.multiple_of(limits[0, o], ALIGN), CAP)
        for b in range(2 * width // LANES):
            out_ref[o, b * CAP : (b + 1) * CAP, :] = ordered[window, b * LANES : (b + 1) * LANES]
        part = ordered[window, 2 * width :].astype(jnp.float32)
        turned = part[:, :LANES].T
        turned = jnp.where(core == 0, turned[:HALF], turned[HALF:])
        out_ref[o, at : at + HALF, :] = turned.astype(jnp.bfloat16)
        tiles = part[:, LANES:].T[:8]
        slots = lax.broadcasted_iota(jnp.int32, tiles.shape, 1)
        tiles = jnp.where(slots < limits[0, 64 + o], tiles, 0.0)
        out_ref[o, at + HALF : at + HALF + 8, :] = tiles.astype(jnp.bfloat16)


def grid_kernel(width, other, in_ref, cols_ref, project_ref, expand_ref, *refs):
    out_ref = refs[-1]
    half = (lax.axis_index("chan") + other) % 2
    senders = in_ref.shape[0]
    blocks = 2 * width // LANES
    at_once = 4
    at = blocks * CAP
    parts = out_ref.shape[0]
    mine = TILES * LANES // parts
    last = width // LANES * mine
    total = None
    for first in range(0, senders, at_once):
        group = range(first, first + at_once)
        spectra = jnp.concatenate(
            [
                jnp.concatenate(
                    [in_ref[s, b * CAP : (b + 1) * CAP, :] for b in range(blocks)], axis=1
                )
                for s in group
            ],
            axis=0,
        )
        columns = []
        for s in group:
            kernel_cols = cols_ref[s]
            tile = in_ref[s, at + HALF : at + HALF + 8, :].astype(jnp.float32)
            pieces = []
            for t in range(TILES):
                here = (tile == float(t + 1)).astype(jnp.float32)
                here = jnp.concatenate([here] * (HALF // 8), axis=0).astype(jnp.bfloat16)
                pieces.append(kernel_cols * here)
            columns.append(jnp.concatenate(pieces, axis=0))
        product = dot(jnp.concatenate(columns, axis=1), spectra)
        total = product if total is None else total + product

    cube = total[:, :width] / (total[:, width:] + 1.0)
    high = cube.astype(jnp.bfloat16)
    low = (cube - high.astype(jnp.float32)).astype(jnp.bfloat16)
    both = dot(high, project_ref[...])
    coef = both[:, :LANES] + (both[:, LANES:] + dot(low, project_ref[:, :LANES]))
    first = coef.astype(jnp.bfloat16).astype(jnp.float32)
    left = coef - first
    second = left.astype(jnp.bfloat16).astype(jnp.float32)
    third = left - second
    group = lax.broadcasted_iota(jnp.int32, coef.shape, 1) // BASIS
    terms = jnp.where(group == 2, third, first)
    terms = jnp.where(jnp.logical_or(group == 1, group == 5), second, terms)
    rest = (cube - dot(terms.astype(jnp.bfloat16), expand_ref[...])).astype(jnp.bfloat16)
    sent = terms.T[:16]
    lane = lax.broadcasted_iota(jnp.int32, (8, LANES), 1)
    for at_pixel in range(0, TILES * HALF, mine):
        c = at_pixel // HALF * (LANES // mine) + half * (HALF // mine) + at_pixel % HALF // mine
        for b in range(width // LANES):
            out_ref[c, b * mine : (b + 1) * mine, :] = rest[
                at_pixel : at_pixel + mine, b * LANES : (b + 1) * LANES
            ]
        here = sent[:, at_pixel // LANES * LANES : at_pixel // LANES * LANES + LANES]
        upper, lower = here[:8], here[8:]
        if at_pixel % LANES:
            upper = pltpu.roll(upper, LANES - at_pixel % LANES, axis=1)
        if at_pixel % LANES != mine:
            lower = pltpu.roll(lower, (LANES + mine - at_pixel % LANES) % LANES, axis=1)
        out_ref[c, last : last + 8, :] = jnp.where(lane < mine, upper, lower).astype(jnp.bfloat16)


def final_kernel(width, in_ref, combine_ref, short_ref, coef_ref, res_ref):
    parts = in_ref.shape[0]
    mine = res_ref.shape[0]
    last = width // LANES * mine
    upper = jnp.concatenate(
        [in_ref[c, last : last + 8, :].astype(jnp.float32) for c in range(parts)], axis=0
    )
    lower = pltpu.roll(upper, LANES - mine, axis=1)
    sent = jnp.concatenate([upper, lower], axis=0).astype(jnp.bfloat16)
    mixed = dot(combine_ref[...], sent)
    size = parts * 8 + 16
    mixed = mixed[:size] + (mixed[size : 2 * size] + mixed[2 * size :])
    coef_ref[...] = mixed[parts * 8 : parts * 8 + BASIS, :mine]
    turned = mixed[: parts * 8].T[:mine]
    high = turned.astype(jnp.bfloat16)
    low = (turned - high.astype(jnp.float32)).astype(jnp.bfloat16)
    both = jnp.concatenate([high, low, high], axis=1)
    owner = lax.broadcasted_iota(jnp.int32, both.shape, 1) % (parts * 8) // 8
    zero = jnp.zeros_like(both)
    spread = jnp.concatenate([jnp.where(owner == c, both, zero) for c in range(parts)], axis=0)
    added = dot(spread, short_ref[...])
    for c in range(parts):
        rest = jnp.concatenate(
            [in_ref[c, b * mine : (b + 1) * mine, :] for b in range(width // LANES)], axis=1
        ).astype(jnp.float32)
        res_ref[:, c * width : (c + 1) * width] = rest + added[c * mine : (c + 1) * mine]


def per_device(owners, parts, spectra, chan_weight, kernel, tile_map, tile_slot):
    count, width = spectra.shape
    mine = TILES * LANES // parts
    project, expand, combine, short = (jnp.asarray(a) for a in tables(CHANNELS, parts))
    limit = pltpu.CompilerParams(vmem_limit_bytes=40 * 2**20)
    hbm = pl.BlockSpec(memory_space=pltpu.HBM)

    long = 2 * width // LANES * CAP + HALF + 8
    room = count + owners * ALIGN
    packed = pl.pallas_call(
        functools.partial(pack_kernel, owners),
        out_shape=jax.ShapeDtypeStruct((owners, long, LANES), jnp.bfloat16),
        in_specs=[hbm] * 5,
        scratch_shapes=[
            pltpu.SMEM(tile_slot.shape, jnp.int32),
            pltpu.VMEM((count // LANES, LANES), jnp.int32),
            pltpu.VMEM((count, 2 * width + 2 * LANES), jnp.bfloat16),
            pltpu.VMEM((room + CAP, 2 * width + 2 * LANES), jnp.bfloat16),
            pltpu.VMEM((8, LANES), jnp.int32),
            pltpu.SMEM((8, LANES), jnp.int32),
            pltpu.SemaphoreType.DMA((6,)),
        ],
        compiler_params=limit,
    )(
        *[
            pltpu.with_memory_space_constraint(a, pltpu.HBM)
            for a in (
                tile_slot,
                tile_map.reshape(count // LANES, LANES),
                spectra,
                chan_weight,
                kernel,
            )
        ]
    )

    routed = lax.all_to_all(packed, "scan", split_axis=0, concat_axis=0, tiled=True)

    tall = width // LANES * mine + 8
    at = 2 * width // LANES * CAP
    mine_cols = routed[:, at : at + HALF, :]
    other_cols = lax.ppermute(mine_cols, "chan", [(c, c ^ 1) for c in range(parts)])
    whole = jax.ShapeDtypeStruct((parts, tall, LANES), jnp.bfloat16)
    vmem = pl.BlockSpec(memory_space=pltpu.VMEM)
    first = pl.pallas_call(
        functools.partial(grid_kernel, width, 0),
        out_shape=whole,
        in_specs=[vmem] * 4,
        out_specs=vmem,
        compiler_params=limit,
        cost_estimate=pl.CostEstimate(flops=10**9, bytes_accessed=3 * 10**6, transcendentals=0),
    )(routed, mine_cols, project, expand)
    gridded = pl.pallas_call(
        functools.partial(grid_kernel, width, 1),
        out_shape=whole,
        in_specs=[vmem] * 5,
        out_specs=vmem,
        input_output_aliases={4: 0},
        compiler_params=limit,
        cost_estimate=pl.CostEstimate(flops=10**9, bytes_accessed=3 * 10**6, transcendentals=0),
    )(routed, other_cols, project, expand, first)

    rows = lax.all_to_all(gridded, "chan", split_axis=0, concat_axis=0, tiled=True)

    return pl.pallas_call(
        functools.partial(final_kernel, width),
        out_shape=[
            jax.ShapeDtypeStruct((BASIS, mine), jnp.float32),
            jax.ShapeDtypeStruct((mine, CHANNELS), jnp.float32),
        ],
        compiler_params=limit,
    )(rows, combine, short)


def solution(mesh):
    placed = (P("scan", "chan"), P("scan", "chan"), P("scan", None), P("scan"), P())
    return jax.shard_map(
        functools.partial(per_device, mesh.shape["scan"], mesh.shape["chan"]),
        mesh=mesh,
        in_specs=placed,
        out_specs=(P(None, ("scan", "chan")), P(("scan", "chan"), None)),
        check_vma=False,
    )
```

```python
import functools

import jax
import jax.numpy as jnp
import numpy as np
from jax import lax
from jax.experimental import pallas as pl
from jax.experimental.pallas import tpu as pltpu
from jax.sharding import PartitionSpec as P

CHANNELS = 4096
BASIS = 5
CAP = 128
TILES = 4
LANES = 128
ALIGN = 16
HALF = LANES // 2


def orthonormal(abscissa, terms):
    columns = []
    for degree in range(terms):
        column = abscissa**degree
        for earlier in columns:
            column = column - np.sum(earlier * column) * earlier
        columns.append(column / np.sqrt(np.sum(column * column)))
    return np.stack(columns, axis=1)


def split_terms(values, terms):
    left = np.asarray(values, np.float64)
    parts = []
    for _ in range(terms):
        part = left.astype(jnp.bfloat16)
        parts.append(part)
        left = left - part.astype(np.float64)
    return parts


LEFT = (0, 1, 2, 0, 0, 1)
RIGHT = (0, 0, 0, 1, 2, 1)


def tables(channels, parts):
    width = channels // parts
    basis = orthonormal((2.0 * np.arange(channels) + 1.0) / channels - 1.0, BASIS)
    local = orthonormal((2.0 * np.arange(width) + 1.0) / width - 1.0, BASIS)
    mix = np.stack([local.T @ basis[c * width : (c + 1) * width] for c in range(parts)])
    project = np.zeros((width, LANES))
    expand = np.zeros((LANES, width), jnp.bfloat16)
    terms = split_terms(local.T, 3)
    for group, term in enumerate(RIGHT):
        project[:, group * BASIS : (group + 1) * BASIS] = local
        expand[group * BASIS : (group + 1) * BASIS] = terms[term]
    project = np.concatenate(split_terms(project, 2), axis=1)
    combine = np.zeros((parts * 8 + 16, parts * 16))
    for c in range(parts):
        for copy in range(3):
            at = c * 16 + copy * BASIS
            combine[parts * 8 : parts * 8 + BASIS, at : at + BASIS] = mix[c].T
            combine[c * 8 : c * 8 + BASIS, at : at + BASIS] += np.eye(BASIS)
    for c in range(parts):
        combine[c * 8 : c * 8 + BASIS] -= mix[c] @ combine[parts * 8 : parts * 8 + BASIS]
    combine = combine.reshape(-1, parts, 2, 8).transpose(0, 2, 1, 3).reshape(-1, parts * 16)
    combine = np.concatenate(split_terms(combine, 3))
    short = np.zeros((parts, 8, width))
    short[:, :BASIS] = local.T
    short = split_terms(short.reshape(parts * 8, width), 2)
    short = np.concatenate([short[0], short[0], short[1]])
    return project, expand, combine, short


def dot(a, b):
    return jnp.dot(a, b, preferred_element_type=jnp.float32)


def one_hot(mask):
    return mask.astype(jnp.float32).astype(jnp.bfloat16)


def pack_kernel(
    owners,
    slot_hbm,
    map_hbm,
    spec_hbm,
    cw_hbm,
    ker_hbm,
    out_ref,
    slot_ref,
    map_ref,
    rows,
    chosen,
    cols,
    ordered,
    bounds,
    limits,
    sems,
):
    core = lax.axis_index("chan") % 2
    groups = map_ref.shape[0]
    width = spec_hbm.shape[1]
    copies = [
        pltpu.make_async_copy(slot_hbm, slot_ref, sems.at[0]),
        pltpu.make_async_copy(map_hbm, map_ref, sems.at[1]),
        pltpu.make_async_copy(ker_hbm, rows.at[:, 2 * width : 2 * width + LANES], sems.at[2]),
        pltpu.make_async_copy(cw_hbm, rows.at[:, width : 2 * width], sems.at[3]),
        pltpu.make_async_copy(spec_hbm, rows.at[:, :width], sems.at[4]),
    ]
    for copy in copies:
        copy.start()
    size = owners * groups
    at0 = lax.broadcasted_iota(jnp.int32, (LANES, LANES), 0)
    at1 = lax.broadcasted_iota(jnp.int32, (LANES, LANES), 1)
    earlier = one_hot(at0 < at1)
    ones = jnp.ones((LANES, LANES), jnp.bfloat16)
    r0 = lax.broadcasted_iota(jnp.int32, (size, size), 0)
    r1 = lax.broadcasted_iota(jnp.int32, (size, size), 1)
    same = r0 // groups == r1 // groups
    above = one_hot(jnp.logical_and(same, r1 < r0))
    before = one_hot(r1 // groups < r0 // groups)
    copies[0].wait()
    copies[1].wait()

    tile_map = map_ref[...]
    slot = jnp.zeros_like(tile_map)
    for t in range(owners * TILES):
        slot = jnp.where(tile_map == t, slot_ref[t], slot)
    owner = slot // TILES
    masks = jnp.concatenate(
        [(owner == o).astype(jnp.float32) for o in range(owners)], axis=0
    ).astype(jnp.bfloat16)
    here = dot(masks, ones).astype(jnp.bfloat16)
    rank = dot(masks, earlier) + dot(above, here)
    count = dot(one_hot(same), here)
    room = jnp.floor((count + (ALIGN - 1.0)) * (1.0 / ALIGN)) * (ALIGN / float(groups))
    begin = dot(before, room.astype(jnp.bfloat16))
    rank = rank + begin
    place = jnp.zeros(owner.shape, jnp.float32)
    for o in range(owners):
        place = jnp.where(owner == o, rank[o * groups : (o + 1) * groups], place)
    place = place.astype(jnp.int32)
    table = jnp.where(at0 == at1 * groups, begin, 0.0)
    table = table + jnp.where(at0 == (at1 - 64) * groups, count, 0.0)
    bounds[...] = jnp.broadcast_to(
        jnp.sum(table, axis=0, keepdims=True), bounds.shape
    ).astype(jnp.int32)
    fetch = pltpu.make_async_copy(bounds, limits, sems.at[5])
    fetch.start()
    tile = (slot - owner * TILES + 1).astype(jnp.float32)
    turned = jnp.concatenate([tile] * (LANES // groups), axis=0).T
    for r in range(groups):
        column = jnp.broadcast_to(turned[:, r : r + 1], (LANES, LANES))
        rows[r * LANES : (r + 1) * LANES, 2 * width + LANES :] = column.astype(jnp.bfloat16)

    total = chosen.shape[0]
    amount = 128
    at = 2 * width // LANES * CAP
    cols[total:, :] = jnp.zeros((CAP, cols.shape[1]), jnp.bfloat16)
    ordered[total:, :] = jnp.zeros((CAP, ordered.shape[1]), jnp.bfloat16)
    copies[2].wait()
    for step in range(total // amount):
        wanted = lax.broadcasted_iota(jnp.int32, (amount, LANES), 0) + step * amount
        picked = jnp.concatenate(
            [one_hot(wanted == place[r : r + 1, :]) for r in range(groups)], axis=1
        )
        here = slice(step * amount, (step + 1) * amount)
        chosen[here, :] = picked
        cols[here, :] = dot(picked, rows[:, 2 * width :]).astype(jnp.bfloat16)
    fetch.wait()
    copies[3].wait()
    copies[4].wait()

    def turn(o):
        window = pl.ds(pl.multiple_of(limits[0, o], ALIGN), CAP)
        part = cols[window, :].astype(jnp.float32)
        turned = part[:, :LANES].T
        turned = jnp.where(core == 0, turned[:HALF], turned[HALF:])
        out_ref[o, at : at + HALF, :] = turned.astype(jnp.bfloat16)
        tiles = part[:, LANES:].T[:8]
        slots = lax.broadcasted_iota(jnp.int32, tiles.shape, 1)
        tiles = jnp.where(slots < limits[0, 64 + o], tiles, 0.0)
        out_ref[o, at + HALF : at + HALF + 8, :] = tiles.astype(jnp.bfloat16)

    steps = total // amount
    for step in range(steps):
        here = slice(step * amount, (step + 1) * amount)
        got = dot(chosen[here, :], rows[:, : 2 * width])
        ordered[here, :width] = (got[:, :width] * got[:, width:]).astype(jnp.bfloat16)
        ordered[here, width:] = got[:, width:].astype(jnp.bfloat16)
        for o in range(step * owners // steps, (step + 1) * owners // steps):
            turn(o)
    for o in range(owners):
        window = pl.ds(pl.multiple_of(limits[0, o], ALIGN), CAP)
        for b in range(2 * width // LANES):
            out_ref[o, b * CAP : (b + 1) * CAP, :] = ordered[window, b * LANES : (b + 1) * LANES]


def grid_kernel(width, other, in_ref, cols_ref, project_ref, expand_ref, *refs):
    out_ref = refs[-1]
    half = (lax.axis_index("chan") + other) % 2
    senders = in_ref.shape[0]
    blocks = 2 * width // LANES
    at_once = 4
    at = blocks * CAP
    parts = out_ref.shape[0]
    mine = TILES * LANES // parts
    last = width // LANES * mine
    total = None
    for first in range(0, senders, at_once):
        group = range(first, first + at_once)
        spectra = jnp.concatenate(
            [
                jnp.concatenate(
                    [in_ref[s, b * CAP : (b + 1) * CAP, :] for b in range(blocks)], axis=1
                )
                for s in group
            ],
            axis=0,
        )
        columns = []
        for s in group:
            kernel_cols = cols_ref[s]
            tile = in_ref[s, at + HALF : at + HALF + 8, :].astype(jnp.float32)
            pieces = []
            for t in range(TILES):
                here = (tile == float(t + 1)).astype(jnp.float32)
                here = jnp.concatenate([here] * (HALF // 8), axis=0).astype(jnp.bfloat16)
                pieces.append(kernel_cols * here)
            columns.append(jnp.concatenate(pieces, axis=0))
        product = dot(jnp.concatenate(columns, axis=1), spectra)
        total = product if total is None else total + product

    cube = total[:, :width] / (total[:, width:] + 1.0)
    high = cube.astype(jnp.bfloat16)
    low = (cube - high.astype(jnp.float32)).astype(jnp.bfloat16)
    both = dot(high, project_ref[...])
    coef = both[:, :LANES] + (both[:, LANES:] + dot(low, project_ref[:, :LANES]))
    first = coef.astype(jnp.bfloat16).astype(jnp.float32)
    left = coef - first
    second = left.astype(jnp.bfloat16).astype(jnp.float32)
    third = left - second
    group = lax.broadcasted_iota(jnp.int32, coef.shape, 1) // BASIS
    terms = jnp.where(group == 2, third, first)
    terms = jnp.where(jnp.logical_or(group == 1, group == 5), second, terms)
    rest = (cube - dot(terms.astype(jnp.bfloat16), expand_ref[...])).astype(jnp.bfloat16)
    sent = terms.T[:16]
    lane = lax.broadcasted_iota(jnp.int32, (8, LANES), 1)
    for at_pixel in range(0, TILES * HALF, mine):
        c = at_pixel // HALF * (LANES // mine) + half * (HALF // mine) + at_pixel % HALF // mine
        for b in range(width // LANES):
            out_ref[c, b * mine : (b + 1) * mine, :] = rest[
                at_pixel : at_pixel + mine, b * LANES : (b + 1) * LANES
            ]
        here = sent[:, at_pixel // LANES * LANES : at_pixel // LANES * LANES + LANES]
        upper, lower = here[:8], here[8:]
        if at_pixel % LANES:
            upper = pltpu.roll(upper, LANES - at_pixel % LANES, axis=1)
        if at_pixel % LANES != mine:
            lower = pltpu.roll(lower, (LANES + mine - at_pixel % LANES) % LANES, axis=1)
        out_ref[c, last : last + 8, :] = jnp.where(lane < mine, upper, lower).astype(jnp.bfloat16)


def final_kernel(
    width, in_ref, combine_ref, short_ref, coef_hbm, res_hbm, coef_ref, res_ref, sems
):
    parts = in_ref.shape[0]
    mine = res_ref.shape[0]
    last = width // LANES * mine
    upper = jnp.concatenate(
        [in_ref[c, last : last + 8, :].astype(jnp.float32) for c in range(parts)], axis=0
    )
    lower = pltpu.roll(upper, LANES - mine, axis=1)
    sent = jnp.concatenate([upper, lower], axis=0).astype(jnp.bfloat16)
    mixed = dot(combine_ref[...], sent)
    size = parts * 8 + 16
    mixed = mixed[:size] + (mixed[size : 2 * size] + mixed[2 * size :])
    coef_ref[...] = mixed[parts * 8 : parts * 8 + BASIS, :mine]
    copies = [pltpu.make_async_copy(coef_ref, coef_hbm, sems.at[0])]
    copies[0].start()
    turned = mixed[: parts * 8].T[:mine]
    high = turned.astype(jnp.bfloat16)
    low = (turned - high.astype(jnp.float32)).astype(jnp.bfloat16)
    both = jnp.concatenate([high, low, high], axis=1)
    owner = lax.broadcasted_iota(jnp.int32, both.shape, 1) % (parts * 8) // 8
    zero = jnp.zeros_like(both)
    pieces = sems.shape[0] - 1
    for piece in range(pieces):
        group = range(piece * parts // pieces, (piece + 1) * parts // pieces)
        spread = jnp.concatenate([jnp.where(owner == c, both, zero) for c in group], axis=0)
        added = dot(spread, short_ref[...])
        for i, c in enumerate(group):
            rest = jnp.concatenate(
                [in_ref[c, b * mine : (b + 1) * mine, :] for b in range(width // LANES)], axis=1
            ).astype(jnp.float32)
            res_ref[:, c * width : (c + 1) * width] = rest + added[i * mine : (i + 1) * mine]
        lanes = slice(group[0] * width, (group[-1] + 1) * width)
        copies.append(
            pltpu.make_async_copy(
                res_ref.at[:, lanes], res_hbm.at[:, lanes], sems.at[piece + 1]
            )
        )
        copies[-1].start()
    for copy in copies:
        copy.wait()


def per_device(owners, parts, spectra, chan_weight, kernel, tile_map, tile_slot):
    count, width = spectra.shape
    mine = TILES * LANES // parts
    project, expand, combine, short = (jnp.asarray(a) for a in tables(CHANNELS, parts))
    limit = pltpu.CompilerParams(vmem_limit_bytes=40 * 2**20)
    hbm = pl.BlockSpec(memory_space=pltpu.HBM)

    long = 2 * width // LANES * CAP + HALF + 8
    room = count + owners * ALIGN
    packed = pl.pallas_call(
        functools.partial(pack_kernel, owners),
        out_shape=jax.ShapeDtypeStruct((owners, long, LANES), jnp.bfloat16),
        in_specs=[hbm] * 5,
        scratch_shapes=[
            pltpu.SMEM(tile_slot.shape, jnp.int32),
            pltpu.VMEM((count // LANES, LANES), jnp.int32),
            pltpu.VMEM((count, 2 * width + 2 * LANES), jnp.bfloat16),
            pltpu.VMEM((room, count), jnp.bfloat16),
            pltpu.VMEM((room + CAP, 2 * LANES), jnp.bfloat16),
            pltpu.VMEM((room + CAP, 2 * width), jnp.bfloat16),
            pltpu.VMEM((8, LANES), jnp.int32),
            pltpu.SMEM((8, LANES), jnp.int32),
            pltpu.SemaphoreType.DMA((6,)),
        ],
        compiler_params=limit,
    )(
        *[
            pltpu.with_memory_space_constraint(a, pltpu.HBM)
            for a in (
                tile_slot,
                tile_map.reshape(count // LANES, LANES),
                spectra,
                chan_weight,
                kernel,
            )
        ]
    )

    routed = lax.all_to_all(packed, "scan", split_axis=0, concat_axis=0, tiled=True)

    tall = width // LANES * mine + 8
    at = 2 * width // LANES * CAP
    mine_cols = routed[:, at : at + HALF, :]
    other_cols = lax.ppermute(mine_cols, "chan", [(c, c ^ 1) for c in range(parts)])
    whole = jax.ShapeDtypeStruct((parts, tall, LANES), jnp.bfloat16)
    vmem = pl.BlockSpec(memory_space=pltpu.VMEM)
    first = pl.pallas_call(
        functools.partial(grid_kernel, width, 0),
        out_shape=whole,
        in_specs=[vmem] * 4,
        out_specs=vmem,
        compiler_params=limit,
        cost_estimate=pl.CostEstimate(flops=10**9, bytes_accessed=3 * 10**6, transcendentals=0),
    )(routed, mine_cols, project, expand)
    gridded = pl.pallas_call(
        functools.partial(grid_kernel, width, 1),
        out_shape=whole,
        in_specs=[vmem] * 5,
        out_specs=vmem,
        input_output_aliases={4: 0},
        compiler_params=limit,
        cost_estimate=pl.CostEstimate(flops=10**9, bytes_accessed=3 * 10**6, transcendentals=0),
    )(routed, other_cols, project, expand, first)

    rows = lax.all_to_all(gridded, "chan", split_axis=0, concat_axis=0, tiled=True)

    return pl.pallas_call(
        functools.partial(final_kernel, width),
        out_shape=[
            jax.ShapeDtypeStruct((BASIS, mine), jnp.float32),
            jax.ShapeDtypeStruct((mine, CHANNELS), jnp.float32),
        ],
        out_specs=[hbm, hbm],
        scratch_shapes=[
            pltpu.VMEM((BASIS, mine), jnp.float32),
            pltpu.VMEM((mine, CHANNELS), jnp.float32),
            pltpu.SemaphoreType.DMA((1 + 4,)),
        ],
        compiler_params=limit,
    )(rows, combine, short)


def solution(mesh):
    placed = (P("scan", "chan"), P("scan", "chan"), P("scan", None), P("scan"), P())
    return jax.shard_map(
        functools.partial(per_device, mesh.shape["scan"], mesh.shape["chan"]),
        mesh=mesh,
        in_specs=placed,
        out_specs=(P(None, ("scan", "chan")), P(("scan", "chan"), None)),
        check_vma=False,
    )
```

```python
import functools

import jax
import jax.numpy as jnp
import numpy as np
from jax import lax
from jax.experimental import pallas as pl
from jax.experimental.pallas import tpu as pltpu
from jax.sharding import PartitionSpec as P

CHANNELS = 4096
BASIS = 5
CAP = 128
TILES = 4
LANES = 128
ALIGN = 16
HALF = LANES // 2


def orthonormal(abscissa, terms):
    columns = []
    for degree in range(terms):
        column = abscissa**degree
        for earlier in columns:
            column = column - np.sum(earlier * column) * earlier
        columns.append(column / np.sqrt(np.sum(column * column)))
    return np.stack(columns, axis=1)


def split_terms(values, terms):
    left = np.asarray(values, np.float64)
    parts = []
    for _ in range(terms):
        part = left.astype(jnp.bfloat16)
        parts.append(part)
        left = left - part.astype(np.float64)
    return parts


LEFT = (0, 1, 2, 0, 0, 1)
RIGHT = (0, 0, 0, 1, 2, 1)


def tables(channels, parts):
    width = channels // parts
    basis = orthonormal((2.0 * np.arange(channels) + 1.0) / channels - 1.0, BASIS)
    local = orthonormal((2.0 * np.arange(width) + 1.0) / width - 1.0, BASIS)
    mix = np.stack([local.T @ basis[c * width : (c + 1) * width] for c in range(parts)])
    project = np.zeros((width, LANES))
    expand = np.zeros((LANES, width), jnp.bfloat16)
    terms = split_terms(local.T, 3)
    for group, term in enumerate(RIGHT):
        project[:, group * BASIS : (group + 1) * BASIS] = local
        expand[group * BASIS : (group + 1) * BASIS] = terms[term]
    project = np.concatenate(split_terms(project, 2), axis=1)
    combine = np.zeros((parts * 8 + LANES, parts * 16))
    for c in range(parts):
        for copy in range(3):
            at = c * 16 + copy * BASIS
            combine[parts * 8 : parts * 8 + BASIS, at : at + BASIS] = mix[c].T
            combine[c * 8 : c * 8 + BASIS, at : at + BASIS] += np.eye(BASIS)
    for c in range(parts):
        combine[c * 8 : c * 8 + BASIS] -= mix[c] @ combine[parts * 8 : parts * 8 + BASIS]
    combine = combine.reshape(-1, parts, 2, 8).transpose(0, 2, 1, 3).reshape(-1, parts * 16)
    combine = np.concatenate(split_terms(combine.T, 3), axis=1)
    short = np.zeros((parts, 8, width))
    short[:, :BASIS] = local.T
    short = split_terms(short.reshape(parts * 8, width), 2)
    short = np.concatenate([short[0], short[0], short[1]])
    return project, expand, combine, short


def dot(a, b):
    return jnp.dot(a, b, preferred_element_type=jnp.float32)


def one_hot(mask):
    return mask.astype(jnp.float32).astype(jnp.bfloat16)


def pack_kernel(
    owners,
    slot_hbm,
    map_hbm,
    spec_hbm,
    cw_hbm,
    ker_hbm,
    out_ref,
    slot_ref,
    map_ref,
    rows,
    chosen,
    cols,
    ordered,
    bounds,
    limits,
    sems,
):
    core = lax.axis_index("chan") % 2
    groups = map_ref.shape[0]
    width = spec_hbm.shape[1]
    copies = [
        pltpu.make_async_copy(slot_hbm, slot_ref, sems.at[0]),
        pltpu.make_async_copy(map_hbm, map_ref, sems.at[1]),
        pltpu.make_async_copy(ker_hbm, rows.at[:, 2 * width : 2 * width + LANES], sems.at[2]),
        pltpu.make_async_copy(cw_hbm, rows.at[:, width : 2 * width], sems.at[3]),
        pltpu.make_async_copy(spec_hbm, rows.at[:, :width], sems.at[4]),
    ]
    for copy in copies:
        copy.start()
    size = owners * groups
    at0 = lax.broadcasted_iota(jnp.int32, (LANES, LANES), 0)
    at1 = lax.broadcasted_iota(jnp.int32, (LANES, LANES), 1)
    earlier = one_hot(at0 < at1)
    ones = jnp.ones((LANES, LANES), jnp.bfloat16)
    r0 = lax.broadcasted_iota(jnp.int32, (size, size), 0)
    r1 = lax.broadcasted_iota(jnp.int32, (size, size), 1)
    same = r0 // groups == r1 // groups
    above = one_hot(jnp.logical_and(same, r1 < r0))
    before = one_hot(r1 // groups < r0 // groups)
    copies[0].wait()
    copies[1].wait()

    tile_map = map_ref[...]
    slot = jnp.zeros_like(tile_map)
    for t in range(owners * TILES):
        slot = jnp.where(tile_map == t, slot_ref[t], slot)
    owner = slot // TILES
    masks = jnp.concatenate(
        [(owner == o).astype(jnp.float32) for o in range(owners)], axis=0
    ).astype(jnp.bfloat16)
    here = dot(masks, ones).astype(jnp.bfloat16)
    rank = dot(masks, earlier) + dot(above, here)
    count = dot(one_hot(same), here)
    room = jnp.floor((count + (ALIGN - 1.0)) * (1.0 / ALIGN)) * (ALIGN / float(groups))
    begin = dot(before, room.astype(jnp.bfloat16))
    rank = rank + begin
    place = jnp.zeros(owner.shape, jnp.float32)
    for o in range(owners):
        place = jnp.where(owner == o, rank[o * groups : (o + 1) * groups], place)
    place = place.astype(jnp.int32)
    table = jnp.where(at0 == at1 * groups, begin, 0.0)
    table = table + jnp.where(at0 == (at1 - 64) * groups, count, 0.0)
    bounds[...] = jnp.broadcast_to(
        jnp.sum(table, axis=0, keepdims=True), bounds.shape
    ).astype(jnp.int32)
    fetch = pltpu.make_async_copy(bounds, limits, sems.at[5])
    fetch.start()
    tile = (slot - owner * TILES + 1).astype(jnp.float32)
    turned = jnp.concatenate([tile] * (LANES // groups), axis=0).T
    for r in range(groups):
        column = jnp.broadcast_to(turned[:, r : r + 1], (LANES, LANES))
        rows[r * LANES : (r + 1) * LANES, 2 * width + LANES :] = column.astype(jnp.bfloat16)

    total = chosen.shape[0]
    amount = 128
    at = 2 * width // LANES * CAP
    cols[total:, :] = jnp.zeros((CAP, cols.shape[1]), jnp.bfloat16)
    ordered[total:, :] = jnp.zeros((CAP, ordered.shape[1]), jnp.bfloat16)
    copies[2].wait()
    for step in range(total // amount):
        wanted = lax.broadcasted_iota(jnp.int32, (amount, LANES), 0) + step * amount
        picked = jnp.concatenate(
            [one_hot(wanted == place[r : r + 1, :]) for r in range(groups)], axis=1
        )
        here = slice(step * amount, (step + 1) * amount)
        chosen[here, :] = picked
        cols[here, :] = dot(picked, rows[:, 2 * width :]).astype(jnp.bfloat16)
    fetch.wait()
    copies[3].wait()
    copies[4].wait()

    def turn(o):
        window = pl.ds(pl.multiple_of(limits[0, o], ALIGN), CAP)
        part = cols[window, :].astype(jnp.float32)
        turned = part[:, :LANES].T
        turned = jnp.where(core == 0, turned[:HALF], turned[HALF:])
        out_ref[o, at : at + HALF, :] = turned.astype(jnp.bfloat16)
        tiles = part[:, LANES:].T[:8]
        slots = lax.broadcasted_iota(jnp.int32, tiles.shape, 1)
        tiles = jnp.where(slots < limits[0, 64 + o], tiles, 0.0)
        out_ref[o, at + HALF : at + HALF + 8, :] = tiles.astype(jnp.bfloat16)

    steps = total // amount
    for step in range(steps):
        here = slice(step * amount, (step + 1) * amount)
        got = dot(chosen[here, :], rows[:, : 2 * width])
        ordered[here, :width] = (got[:, :width] * got[:, width:]).astype(jnp.bfloat16)
        ordered[here, width:] = got[:, width:].astype(jnp.bfloat16)
        for o in range(step * owners // steps, (step + 1) * owners // steps):
            turn(o)
    for o in range(owners):
        window = pl.ds(pl.multiple_of(limits[0, o], ALIGN), CAP)
        for b in range(2 * width // LANES):
            out_ref[o, b * CAP : (b + 1) * CAP, :] = ordered[window, b * LANES : (b + 1) * LANES]


def grid_kernel(width, other, in_ref, cols_ref, project_ref, expand_ref, *refs):
    out_ref = refs[-1]
    half = (lax.axis_index("chan") + other) % 2
    senders = in_ref.shape[0]
    blocks = 2 * width // LANES
    at_once = 4
    at = blocks * CAP
    parts = out_ref.shape[0]
    mine = TILES * LANES // parts
    last = width // LANES * mine
    total = None
    for first in range(0, senders, at_once):
        group = range(first, first + at_once)
        spectra = jnp.concatenate(
            [
                jnp.concatenate(
                    [in_ref[s, b * CAP : (b + 1) * CAP, :] for b in range(blocks)], axis=1
                )
                for s in group
            ],
            axis=0,
        )
        columns = []
        for s in group:
            kernel_cols = cols_ref[s]
            tile = in_ref[s, at + HALF : at + HALF + 8, :].astype(jnp.float32)
            pieces = []
            for t in range(TILES):
                here = (tile == float(t + 1)).astype(jnp.float32)
                here = jnp.concatenate([here] * (HALF // 8), axis=0).astype(jnp.bfloat16)
                pieces.append(kernel_cols * here)
            columns.append(jnp.concatenate(pieces, axis=0))
        product = dot(jnp.concatenate(columns, axis=1), spectra)
        total = product if total is None else total + product

    cube = total[:, :width] / (total[:, width:] + 1.0)
    high = cube.astype(jnp.bfloat16)
    low = (cube - high.astype(jnp.float32)).astype(jnp.bfloat16)
    both = dot(high, project_ref[...])
    coef = both[:, :LANES] + (both[:, LANES:] + dot(low, project_ref[:, :LANES]))
    first = coef.astype(jnp.bfloat16).astype(jnp.float32)
    left = coef - first
    second = left.astype(jnp.bfloat16).astype(jnp.float32)
    third = left - second
    group = lax.broadcasted_iota(jnp.int32, coef.shape, 1) // BASIS
    terms = jnp.where(group == 2, third, first)
    terms = jnp.where(jnp.logical_or(group == 1, group == 5), second, terms)
    rest = (cube - dot(terms.astype(jnp.bfloat16), expand_ref[...])).astype(jnp.bfloat16)
    sent = terms.T[:16]
    lane = lax.broadcasted_iota(jnp.int32, (8, LANES), 1)
    for at_pixel in range(0, TILES * HALF, mine):
        c = at_pixel // HALF * (LANES // mine) + half * (HALF // mine) + at_pixel % HALF // mine
        for b in range(width // LANES):
            out_ref[c, b * mine : (b + 1) * mine, :] = rest[
                at_pixel : at_pixel + mine, b * LANES : (b + 1) * LANES
            ]
        here = sent[:, at_pixel // LANES * LANES : at_pixel // LANES * LANES + LANES]
        upper, lower = here[:8], here[8:]
        if at_pixel % LANES:
            upper = pltpu.roll(upper, LANES - at_pixel % LANES, axis=1)
        if at_pixel % LANES != mine:
            lower = pltpu.roll(lower, (LANES + mine - at_pixel % LANES) % LANES, axis=1)
        out_ref[c, last : last + 8, :] = jnp.where(lane < mine, upper, lower).astype(jnp.bfloat16)


def final_kernel(
    width, in_ref, combine_ref, short_ref, coef_hbm, res_hbm, coef_ref, res_ref, sems
):
    parts = in_ref.shape[0]
    mine = res_ref.shape[0]
    last = width // LANES * mine
    upper = jnp.concatenate(
        [in_ref[c, last : last + 8, :].astype(jnp.float32) for c in range(parts)], axis=0
    )
    turned = upper.T
    sent = jnp.concatenate([turned[:mine], turned[mine : 2 * mine]], axis=1).astype(jnp.bfloat16)
    mixed = dot(sent, combine_ref[...])
    size = combine_ref.shape[1] // 3
    mixed = mixed[:, :size] + (mixed[:, size : 2 * size] + mixed[:, 2 * size :])
    coef_ref[...] = mixed[:, parts * 8 :].T[:BASIS]
    copies = [pltpu.make_async_copy(coef_ref, coef_hbm, sems.at[0])]
    copies[0].start()
    turned = mixed[:, : parts * 8]
    high = turned.astype(jnp.bfloat16)
    low = (turned - high.astype(jnp.float32)).astype(jnp.bfloat16)
    both = jnp.concatenate([high, low, high], axis=1)
    owner = lax.broadcasted_iota(jnp.int32, both.shape, 1) % (parts * 8) // 8
    zero = jnp.zeros_like(both)
    pieces = sems.shape[0] - 1
    for piece in range(pieces):
        group = range(piece * parts // pieces, (piece + 1) * parts // pieces)
        spread = jnp.concatenate([jnp.where(owner == c, both, zero) for c in group], axis=0)
        added = dot(spread, short_ref[...])
        for i, c in enumerate(group):
            rest = jnp.concatenate(
                [in_ref[c, b * mine : (b + 1) * mine, :] for b in range(width // LANES)], axis=1
            ).astype(jnp.float32)
            res_ref[:, c * width : (c + 1) * width] = rest + added[i * mine : (i + 1) * mine]
        lanes = slice(group[0] * width, (group[-1] + 1) * width)
        copies.append(
            pltpu.make_async_copy(
                res_ref.at[:, lanes], res_hbm.at[:, lanes], sems.at[piece + 1]
            )
        )
        copies[-1].start()
    for copy in copies:
        copy.wait()


def per_device(owners, parts, spectra, chan_weight, kernel, tile_map, tile_slot):
    count, width = spectra.shape
    mine = TILES * LANES // parts
    project, expand, combine, short = (jnp.asarray(a) for a in tables(CHANNELS, parts))
    limit = pltpu.CompilerParams(vmem_limit_bytes=40 * 2**20)
    hbm = pl.BlockSpec(memory_space=pltpu.HBM)

    long = 2 * width // LANES * CAP + HALF + 8
    room = count + owners * ALIGN
    packed = pl.pallas_call(
        functools.partial(pack_kernel, owners),
        out_shape=jax.ShapeDtypeStruct((owners, long, LANES), jnp.bfloat16),
        in_specs=[hbm] * 5,
        scratch_shapes=[
            pltpu.SMEM(tile_slot.shape, jnp.int32),
            pltpu.VMEM((count // LANES, LANES), jnp.int32),
            pltpu.VMEM((count, 2 * width + 2 * LANES), jnp.bfloat16),
            pltpu.VMEM((room, count), jnp.bfloat16),
            pltpu.VMEM((room + CAP, 2 * LANES), jnp.bfloat16),
            pltpu.VMEM((room + CAP, 2 * width), jnp.bfloat16),
            pltpu.VMEM((8, LANES), jnp.int32),
            pltpu.SMEM((8, LANES), jnp.int32),
            pltpu.SemaphoreType.DMA((6,)),
        ],
        compiler_params=limit,
    )(
        *[
            pltpu.with_memory_space_constraint(a, pltpu.HBM)
            for a in (
                tile_slot,
                tile_map.reshape(count // LANES, LANES),
                spectra,
                chan_weight,
                kernel,
            )
        ]
    )

    routed = lax.all_to_all(packed, "scan", split_axis=0, concat_axis=0, tiled=True)

    tall = width // LANES * mine + 8
    at = 2 * width // LANES * CAP
    mine_cols = routed[:, at : at + HALF, :]
    other_cols = lax.ppermute(mine_cols, "chan", [(c, c ^ 1) for c in range(parts)])
    whole = jax.ShapeDtypeStruct((parts, tall, LANES), jnp.bfloat16)
    vmem = pl.BlockSpec(memory_space=pltpu.VMEM)
    first = pl.pallas_call(
        functools.partial(grid_kernel, width, 0),
        out_shape=whole,
        in_specs=[vmem] * 4,
        out_specs=vmem,
        compiler_params=limit,
        cost_estimate=pl.CostEstimate(flops=10**9, bytes_accessed=3 * 10**6, transcendentals=0),
    )(routed, mine_cols, project, expand)
    gridded = pl.pallas_call(
        functools.partial(grid_kernel, width, 1),
        out_shape=whole,
        in_specs=[vmem] * 5,
        out_specs=vmem,
        input_output_aliases={4: 0},
        compiler_params=limit,
        cost_estimate=pl.CostEstimate(flops=10**9, bytes_accessed=3 * 10**6, transcendentals=0),
    )(routed, other_cols, project, expand, first)

    rows = lax.all_to_all(gridded, "chan", split_axis=0, concat_axis=0, tiled=True)

    return pl.pallas_call(
        functools.partial(final_kernel, width),
        out_shape=[
            jax.ShapeDtypeStruct((BASIS, mine), jnp.float32),
            jax.ShapeDtypeStruct((mine, CHANNELS), jnp.float32),
        ],
        out_specs=[hbm, hbm],
        scratch_shapes=[
            pltpu.VMEM((BASIS, mine), jnp.float32),
            pltpu.VMEM((mine, CHANNELS), jnp.float32),
            pltpu.SemaphoreType.DMA((1 + 4,)),
        ],
        compiler_params=limit,
    )(rows, combine, short)


def solution(mesh):
    placed = (P("scan", "chan"), P("scan", "chan"), P("scan", None), P("scan"), P())
    return jax.shard_map(
        functools.partial(per_device, mesh.shape["scan"], mesh.shape["chan"]),
        mesh=mesh,
        in_specs=placed,
        out_specs=(P(None, ("scan", "chan")), P(("scan", "chan"), None)),
        check_vma=False,
    )
```

```python
import functools

import jax
import jax.numpy as jnp
import numpy as np
from jax import lax
from jax.experimental import pallas as pl
from jax.experimental.pallas import tpu as pltpu
from jax.sharding import PartitionSpec as P

CHANNELS = 4096
BASIS = 5
CAP = 128
TILES = 4
LANES = 128
ALIGN = 16
HALF = LANES // 2


def orthonormal(abscissa, terms):
    columns = []
    for degree in range(terms):
        column = abscissa**degree
        for earlier in columns:
            column = column - np.sum(earlier * column) * earlier
        columns.append(column / np.sqrt(np.sum(column * column)))
    return np.stack(columns, axis=1)


def split_terms(values, terms):
    left = np.asarray(values, np.float64)
    parts = []
    for _ in range(terms):
        part = left.astype(jnp.bfloat16)
        parts.append(part)
        left = left - part.astype(np.float64)
    return parts


LEFT = (0, 1, 2, 0, 0, 1)
RIGHT = (0, 0, 0, 1, 2, 1)


def tables(channels, parts):
    width = channels // parts
    basis = orthonormal((2.0 * np.arange(channels) + 1.0) / channels - 1.0, BASIS)
    local = orthonormal((2.0 * np.arange(width) + 1.0) / width - 1.0, BASIS)
    mix = np.stack([local.T @ basis[c * width : (c + 1) * width] for c in range(parts)])
    project = np.zeros((width, LANES))
    expand = np.zeros((LANES, width), jnp.bfloat16)
    terms = split_terms(local.T, 3)
    for group, term in enumerate(RIGHT):
        project[:, group * BASIS : (group + 1) * BASIS] = local
        expand[group * BASIS : (group + 1) * BASIS] = terms[term]
    project = np.concatenate(split_terms(project, 2), axis=1)
    combine = np.zeros((parts * 8 + LANES, parts * 16))
    for c in range(parts):
        for copy in range(3):
            at = c * 16 + copy * BASIS
            combine[parts * 8 : parts * 8 + BASIS, at : at + BASIS] = mix[c].T
            combine[c * 8 : c * 8 + BASIS, at : at + BASIS] += np.eye(BASIS)
    for c in range(parts):
        combine[c * 8 : c * 8 + BASIS] -= mix[c] @ combine[parts * 8 : parts * 8 + BASIS]
    combine = combine.reshape(-1, parts, 2, 8).transpose(0, 2, 1, 3).reshape(-1, parts * 16)
    combine = np.concatenate(split_terms(combine.T, 3), axis=1)
    short = np.zeros((parts, 8, width))
    short[:, :BASIS] = local.T
    short = split_terms(short.reshape(parts * 8, width), 2)
    short = np.concatenate([short[0], short[0], short[1]])
    return project, expand, combine, short


def dot(a, b):
    return jnp.dot(a, b, preferred_element_type=jnp.float32)


def one_hot(mask):
    return mask.astype(jnp.float32).astype(jnp.bfloat16)


def pack_kernel(
    owners,
    slot_hbm,
    map_hbm,
    spec_hbm,
    cw_hbm,
    ker_hbm,
    out_ref,
    slot_ref,
    map_ref,
    rows,
    chosen,
    cols,
    ordered,
    bounds,
    limits,
    sems,
):
    core = lax.axis_index("chan") % 2
    groups = map_ref.shape[0]
    width = spec_hbm.shape[1]
    copies = [
        pltpu.make_async_copy(slot_hbm, slot_ref, sems.at[0]),
        pltpu.make_async_copy(map_hbm, map_ref, sems.at[1]),
        pltpu.make_async_copy(ker_hbm, rows.at[:, 2 * width : 2 * width + LANES], sems.at[2]),
        pltpu.make_async_copy(cw_hbm, rows.at[:, width : 2 * width], sems.at[3]),
        pltpu.make_async_copy(spec_hbm, rows.at[:, :width], sems.at[4]),
    ]
    for copy in copies:
        copy.start()
    size = owners * groups
    at0 = lax.broadcasted_iota(jnp.int32, (LANES, LANES), 0)
    at1 = lax.broadcasted_iota(jnp.int32, (LANES, LANES), 1)
    earlier = one_hot(at0 < at1)
    ones = jnp.ones((LANES, LANES), jnp.bfloat16)
    r0 = lax.broadcasted_iota(jnp.int32, (size, size), 0)
    r1 = lax.broadcasted_iota(jnp.int32, (size, size), 1)
    same = r0 // groups == r1 // groups
    above = one_hot(jnp.logical_and(same, r1 < r0))
    before = one_hot(r1 // groups < r0 // groups)
    copies[0].wait()
    copies[1].wait()

    tile_map = map_ref[...]
    table = jnp.concatenate([slot_ref[...], jnp.zeros_like(slot_ref[...])], axis=1)
    table = jnp.broadcast_to(table, tile_map.shape)
    slot = jnp.take_along_axis(table, tile_map, axis=1, mode="promise_in_bounds")
    owner = slot // TILES
    masks = jnp.concatenate(
        [(owner == o).astype(jnp.float32) for o in range(owners)], axis=0
    ).astype(jnp.bfloat16)
    here = dot(masks, ones).astype(jnp.bfloat16)
    rank = dot(masks, earlier) + dot(above, here)
    count = dot(one_hot(same), here)
    room = jnp.floor((count + (ALIGN - 1.0)) * (1.0 / ALIGN)) * (ALIGN / float(groups))
    begin = dot(before, room.astype(jnp.bfloat16))
    rank = rank + begin
    place = jnp.zeros(owner.shape, jnp.float32)
    for o in range(owners):
        place = jnp.where(owner == o, rank[o * groups : (o + 1) * groups], place)
    place = place.astype(jnp.int32)
    table = jnp.where(at0 == at1 * groups, begin, 0.0)
    table = table + jnp.where(at0 == (at1 - 64) * groups, count, 0.0)
    bounds[...] = jnp.broadcast_to(
        jnp.sum(table, axis=0, keepdims=True), bounds.shape
    ).astype(jnp.int32)
    fetch = pltpu.make_async_copy(bounds, limits, sems.at[5])
    fetch.start()
    tile = (slot - owner * TILES + 1).astype(jnp.float32)
    turned = jnp.concatenate([tile] * (LANES // groups), axis=0).T
    for r in range(groups):
        column = jnp.broadcast_to(turned[:, r : r + 1], (LANES, LANES))
        rows[r * LANES : (r + 1) * LANES, 2 * width + LANES :] = column.astype(jnp.bfloat16)

    total = chosen.shape[0]
    amount = 128
    at = 2 * width // LANES * CAP
    cols[total:, :] = jnp.zeros((CAP, cols.shape[1]), jnp.bfloat16)
    ordered[total:, :] = jnp.zeros((CAP, ordered.shape[1]), jnp.bfloat16)
    copies[2].wait()
    for step in range(total // amount):
        wanted = lax.broadcasted_iota(jnp.int32, (amount, LANES), 0) + step * amount
        picked = jnp.concatenate(
            [one_hot(wanted == place[r : r + 1, :]) for r in range(groups)], axis=1
        )
        here = slice(step * amount, (step + 1) * amount)
        chosen[here, :] = picked
        cols[here, :] = dot(picked, rows[:, 2 * width :]).astype(jnp.bfloat16)
    fetch.wait()
    copies[3].wait()
    copies[4].wait()

    def turn(o):
        window = pl.ds(pl.multiple_of(limits[0, o], ALIGN), CAP)
        part = cols[window, :].astype(jnp.float32)
        turned = part[:, :LANES].T
        turned = jnp.where(core == 0, turned[:HALF], turned[HALF:])
        out_ref[o, at : at + HALF, :] = turned.astype(jnp.bfloat16)
        tiles = part[:, LANES:].T[:8]
        slots = lax.broadcasted_iota(jnp.int32, tiles.shape, 1)
        tiles = jnp.where(slots < limits[0, 64 + o], tiles, 0.0)
        out_ref[o, at + HALF : at + HALF + 8, :] = tiles.astype(jnp.bfloat16)

    steps = total // amount
    for step in range(steps):
        here = slice(step * amount, (step + 1) * amount)
        got = dot(chosen[here, :], rows[:, : 2 * width])
        ordered[here, :width] = (got[:, :width] * got[:, width:]).astype(jnp.bfloat16)
        ordered[here, width:] = got[:, width:].astype(jnp.bfloat16)
        for o in range(step * owners // steps, (step + 1) * owners // steps):
            turn(o)
    for o in range(owners):
        window = pl.ds(pl.multiple_of(limits[0, o], ALIGN), CAP)
        for b in range(2 * width // LANES):
            out_ref[o, b * CAP : (b + 1) * CAP, :] = ordered[window, b * LANES : (b + 1) * LANES]


def grid_kernel(width, other, in_ref, cols_ref, project_ref, expand_ref, *refs):
    out_ref = refs[-1]
    half = (lax.axis_index("chan") + other) % 2
    senders = in_ref.shape[0]
    blocks = 2 * width // LANES
    at_once = 4
    at = blocks * CAP
    parts = out_ref.shape[0]
    mine = TILES * LANES // parts
    last = width // LANES * mine
    total = None
    for first in range(0, senders, at_once):
        group = range(first, first + at_once)
        spectra = jnp.concatenate(
            [
                jnp.concatenate(
                    [in_ref[s, b * CAP : (b + 1) * CAP, :] for b in range(blocks)], axis=1
                )
                for s in group
            ],
            axis=0,
        )
        columns = []
        for s in group:
            kernel_cols = cols_ref[s]
            tile = in_ref[s, at + HALF : at + HALF + 8, :].astype(jnp.float32)
            pieces = []
            for t in range(TILES):
                here = (tile == float(t + 1)).astype(jnp.float32)
                here = jnp.concatenate([here] * (HALF // 8), axis=0).astype(jnp.bfloat16)
                pieces.append(kernel_cols * here)
            columns.append(jnp.concatenate(pieces, axis=0))
        product = dot(jnp.concatenate(columns, axis=1), spectra)
        total = product if total is None else total + product

    cube = total[:, :width] / (total[:, width:] + 1.0)
    high = cube.astype(jnp.bfloat16)
    low = (cube - high.astype(jnp.float32)).astype(jnp.bfloat16)
    both = dot(high, project_ref[...])
    coef = both[:, :LANES] + (both[:, LANES:] + dot(low, project_ref[:, :LANES]))
    first = coef.astype(jnp.bfloat16).astype(jnp.float32)
    left = coef - first
    second = left.astype(jnp.bfloat16).astype(jnp.float32)
    third = left - second
    group = lax.broadcasted_iota(jnp.int32, coef.shape, 1) // BASIS
    terms = jnp.where(group == 2, third, first)
    terms = jnp.where(jnp.logical_or(group == 1, group == 5), second, terms)
    rest = (cube - dot(terms.astype(jnp.bfloat16), expand_ref[...])).astype(jnp.bfloat16)
    sent = terms.T[:16]
    lane = lax.broadcasted_iota(jnp.int32, (8, LANES), 1)
    for at_pixel in range(0, TILES * HALF, mine):
        c = at_pixel // HALF * (LANES // mine) + half * (HALF // mine) + at_pixel % HALF // mine
        for b in range(width // LANES):
            out_ref[c, b * mine : (b + 1) * mine, :] = rest[
                at_pixel : at_pixel + mine, b * LANES : (b + 1) * LANES
            ]
        here = sent[:, at_pixel // LANES * LANES : at_pixel // LANES * LANES + LANES]
        upper, lower = here[:8], here[8:]
        if at_pixel % LANES:
            upper = pltpu.roll(upper, LANES - at_pixel % LANES, axis=1)
        if at_pixel % LANES != mine:
            lower = pltpu.roll(lower, (LANES + mine - at_pixel % LANES) % LANES, axis=1)
        out_ref[c, last : last + 8, :] = jnp.where(lane < mine, upper, lower).astype(jnp.bfloat16)


def final_kernel(
    width, in_ref, combine_ref, short_ref, coef_hbm, res_hbm, coef_ref, res_ref, sems
):
    parts = in_ref.shape[0]
    mine = res_ref.shape[0]
    last = width // LANES * mine
    upper = jnp.concatenate(
        [in_ref[c, last : last + 8, :].astype(jnp.float32) for c in range(parts)], axis=0
    )
    turned = upper.T
    sent = jnp.concatenate([turned[:mine], turned[mine : 2 * mine]], axis=1).astype(jnp.bfloat16)
    mixed = dot(sent, combine_ref[...])
    size = combine_ref.shape[1] // 3
    mixed = mixed[:, :size] + (mixed[:, size : 2 * size] + mixed[:, 2 * size :])
    coef_ref[...] = mixed[:, parts * 8 :].T[:BASIS]
    copies = [pltpu.make_async_copy(coef_ref, coef_hbm, sems.at[0])]
    copies[0].start()
    turned = mixed[:, : parts * 8]
    high = turned.astype(jnp.bfloat16)
    low = (turned - high.astype(jnp.float32)).astype(jnp.bfloat16)
    owner = lax.broadcasted_iota(jnp.int32, high.shape, 1) // 8
    zero = jnp.zeros_like(high)
    pieces = sems.shape[0] - 1
    for piece in range(pieces):
        group = range(piece * parts // pieces, (piece + 1) * parts // pieces)
        highs = jnp.concatenate([jnp.where(owner == c, high, zero) for c in group], axis=0)
        lows = jnp.concatenate([jnp.where(owner == c, low, zero) for c in group], axis=0)
        added = dot(jnp.concatenate([highs, lows, highs], axis=1), short_ref[...])
        for i, c in enumerate(group):
            rest = jnp.concatenate(
                [in_ref[c, b * mine : (b + 1) * mine, :] for b in range(width // LANES)], axis=1
            ).astype(jnp.float32)
            res_ref[:, c * width : (c + 1) * width] = rest + added[i * mine : (i + 1) * mine]
        lanes = slice(group[0] * width, (group[-1] + 1) * width)
        copies.append(
            pltpu.make_async_copy(
                res_ref.at[:, lanes], res_hbm.at[:, lanes], sems.at[piece + 1]
            )
        )
        copies[-1].start()
    for copy in copies:
        copy.wait()


def per_device(owners, parts, spectra, chan_weight, kernel, tile_map, tile_slot):
    count, width = spectra.shape
    mine = TILES * LANES // parts
    project, expand, combine, short = (jnp.asarray(a) for a in tables(CHANNELS, parts))
    limit = pltpu.CompilerParams(vmem_limit_bytes=40 * 2**20)
    hbm = pl.BlockSpec(memory_space=pltpu.HBM)

    long = 2 * width // LANES * CAP + HALF + 8
    room = count + owners * ALIGN
    packed = pl.pallas_call(
        functools.partial(pack_kernel, owners),
        out_shape=jax.ShapeDtypeStruct((owners, long, LANES), jnp.bfloat16),
        in_specs=[hbm] * 5,
        scratch_shapes=[
            pltpu.VMEM((1, tile_slot.shape[0]), jnp.int32),
            pltpu.VMEM((count // LANES, LANES), jnp.int32),
            pltpu.VMEM((count, 2 * width + 2 * LANES), jnp.bfloat16),
            pltpu.VMEM((room, count), jnp.bfloat16),
            pltpu.VMEM((room + CAP, 2 * LANES), jnp.bfloat16),
            pltpu.VMEM((room + CAP, 2 * width), jnp.bfloat16),
            pltpu.VMEM((8, LANES), jnp.int32),
            pltpu.SMEM((8, LANES), jnp.int32),
            pltpu.SemaphoreType.DMA((6,)),
        ],
        compiler_params=limit,
    )(
        *[
            pltpu.with_memory_space_constraint(a, pltpu.HBM)
            for a in (
                tile_slot.reshape(1, -1),
                tile_map.reshape(count // LANES, LANES),
                spectra,
                chan_weight,
                kernel,
            )
        ]
    )

    routed = lax.all_to_all(packed, "scan", split_axis=0, concat_axis=0, tiled=True)

    tall = width // LANES * mine + 8
    at = 2 * width // LANES * CAP
    mine_cols = routed[:, at : at + HALF, :]
    other_cols = lax.ppermute(mine_cols, "chan", [(c, c ^ 1) for c in range(parts)])
    whole = jax.ShapeDtypeStruct((parts, tall, LANES), jnp.bfloat16)
    vmem = pl.BlockSpec(memory_space=pltpu.VMEM)
    first = pl.pallas_call(
        functools.partial(grid_kernel, width, 0),
        out_shape=whole,
        in_specs=[vmem] * 4,
        out_specs=vmem,
        compiler_params=limit,
        cost_estimate=pl.CostEstimate(flops=10**9, bytes_accessed=3 * 10**6, transcendentals=0),
    )(routed, mine_cols, project, expand)
    gridded = pl.pallas_call(
        functools.partial(grid_kernel, width, 1),
        out_shape=whole,
        in_specs=[vmem] * 5,
        out_specs=vmem,
        input_output_aliases={4: 0},
        compiler_params=limit,
        cost_estimate=pl.CostEstimate(flops=10**9, bytes_accessed=3 * 10**6, transcendentals=0),
    )(routed, other_cols, project, expand, first)

    rows = lax.all_to_all(gridded, "chan", split_axis=0, concat_axis=0, tiled=True)

    return pl.pallas_call(
        functools.partial(final_kernel, width),
        out_shape=[
            jax.ShapeDtypeStruct((BASIS, mine), jnp.float32),
            jax.ShapeDtypeStruct((mine, CHANNELS), jnp.float32),
        ],
        out_specs=[hbm, hbm],
        scratch_shapes=[
            pltpu.VMEM((BASIS, mine), jnp.float32),
            pltpu.VMEM((mine, CHANNELS), jnp.float32),
            pltpu.SemaphoreType.DMA((1 + 4,)),
        ],
        compiler_params=limit,
    )(rows, combine, short)


def solution(mesh):
    placed = (P("scan", "chan"), P("scan", "chan"), P("scan", None), P("scan"), P())
    return jax.shard_map(
        functools.partial(per_device, mesh.shape["scan"], mesh.shape["chan"]),
        mesh=mesh,
        in_specs=placed,
        out_specs=(P(None, ("scan", "chan")), P(("scan", "chan"), None)),
        check_vma=False,
    )
```

```python
import functools

import jax
import jax.numpy as jnp
import numpy as np
from jax import lax
from jax.experimental import pallas as pl
from jax.experimental.pallas import tpu as pltpu
from jax.sharding import PartitionSpec as P

CHANNELS = 4096
BASIS = 5
CAP = 128
TILES = 4
LANES = 128
ALIGN = 16
HALF = LANES // 2


def orthonormal(abscissa, terms):
    columns = []
    for degree in range(terms):
        column = abscissa**degree
        for earlier in columns:
            column = column - np.sum(earlier * column) * earlier
        columns.append(column / np.sqrt(np.sum(column * column)))
    return np.stack(columns, axis=1)


def split_terms(values, terms):
    left = np.asarray(values, np.float64)
    parts = []
    for _ in range(terms):
        part = left.astype(jnp.bfloat16)
        parts.append(part)
        left = left - part.astype(np.float64)
    return parts


LEFT = (0, 1, 2, 0, 0, 1)
RIGHT = (0, 0, 0, 1, 2, 1)


def tables(channels, parts):
    width = channels // parts
    basis = orthonormal((2.0 * np.arange(channels) + 1.0) / channels - 1.0, BASIS)
    local = orthonormal((2.0 * np.arange(width) + 1.0) / width - 1.0, BASIS)
    mix = np.stack([local.T @ basis[c * width : (c + 1) * width] for c in range(parts)])
    project = np.zeros((width, LANES))
    expand = np.zeros((LANES, width), jnp.bfloat16)
    terms = split_terms(local.T, 3)
    for group, term in enumerate(RIGHT):
        project[:, group * BASIS : (group + 1) * BASIS] = local
        expand[group * BASIS : (group + 1) * BASIS] = terms[term]
    project = np.concatenate(split_terms(project, 2), axis=1)
    combine = np.zeros((parts * 8 + LANES, parts * 16))
    for c in range(parts):
        for copy in range(3):
            at = c * 16 + copy * BASIS
            combine[parts * 8 : parts * 8 + BASIS, at : at + BASIS] = mix[c].T
            combine[c * 8 : c * 8 + BASIS, at : at + BASIS] += np.eye(BASIS)
    for c in range(parts):
        combine[c * 8 : c * 8 + BASIS] -= mix[c] @ combine[parts * 8 : parts * 8 + BASIS]
    combine = combine.reshape(-1, parts, 2, 8).transpose(0, 2, 1, 3).reshape(-1, parts * 16)
    combine = np.concatenate(split_terms(combine.T, 3), axis=1)
    short = np.zeros((parts, 8, width))
    short[:, :BASIS] = local.T
    short = split_terms(short.reshape(parts * 8, width), 2)
    short = np.concatenate([short[0], short[0], short[1]])
    return project, expand, combine, short


def dot(a, b):
    return jnp.dot(a, b, preferred_element_type=jnp.float32)


def one_hot(mask):
    return mask.astype(jnp.float32).astype(jnp.bfloat16)


def pack_kernel(
    owners,
    slot_hbm,
    map_hbm,
    spec_hbm,
    cw_hbm,
    ker_hbm,
    out_ref,
    slot_ref,
    map_ref,
    rows,
    chosen,
    cols,
    ordered,
    bounds,
    limits,
    sems,
):
    core = lax.axis_index("chan") % 2
    groups = map_ref.shape[0]
    width = spec_hbm.shape[1]
    copies = [
        pltpu.make_async_copy(slot_hbm, slot_ref, sems.at[0]),
        pltpu.make_async_copy(map_hbm, map_ref, sems.at[1]),
        pltpu.make_async_copy(ker_hbm, rows.at[:, 2 * width : 2 * width + LANES], sems.at[2]),
        pltpu.make_async_copy(cw_hbm, rows.at[:, width : 2 * width], sems.at[3]),
        pltpu.make_async_copy(spec_hbm, rows.at[:, :width], sems.at[4]),
    ]
    for copy in copies:
        copy.start()
    size = owners * groups
    at0 = lax.broadcasted_iota(jnp.int32, (LANES, LANES), 0)
    at1 = lax.broadcasted_iota(jnp.int32, (LANES, LANES), 1)
    earlier = one_hot(at0 < at1)
    ones = jnp.ones((LANES, LANES), jnp.bfloat16)
    r0 = lax.broadcasted_iota(jnp.int32, (size, size), 0)
    r1 = lax.broadcasted_iota(jnp.int32, (size, size), 1)
    same = r0 // groups == r1 // groups
    above = one_hot(jnp.logical_and(same, r1 < r0))
    before = one_hot(r1 // groups < r0 // groups)
    copies[0].wait()
    copies[1].wait()

    tile_map = map_ref[...]
    table = jnp.concatenate([slot_ref[...], jnp.zeros_like(slot_ref[...])], axis=1)
    table = jnp.broadcast_to(table, tile_map.shape)
    slot = jnp.take_along_axis(table, tile_map, axis=1, mode="promise_in_bounds")
    owner = slot // TILES
    masks = jnp.concatenate(
        [(owner == o).astype(jnp.float32) for o in range(owners)], axis=0
    ).astype(jnp.bfloat16)
    here = dot(masks, ones).astype(jnp.bfloat16)
    rank = dot(masks, earlier) + dot(above, here)
    count = dot(one_hot(same), here)
    room = jnp.floor((count + (ALIGN - 1.0)) * (1.0 / ALIGN)) * (ALIGN / float(groups))
    begin = dot(before, room.astype(jnp.bfloat16))
    rank = rank + begin
    place = jnp.zeros(owner.shape, jnp.float32)
    for o in range(owners):
        place = jnp.where(owner == o, rank[o * groups : (o + 1) * groups], place)
    place = place.astype(jnp.int32)
    table = jnp.where(at0 == at1 * groups, begin, 0.0)
    table = table + jnp.where(at0 == (at1 - 64) * groups, count, 0.0)
    bounds[...] = jnp.broadcast_to(
        jnp.sum(table, axis=0, keepdims=True), bounds.shape
    ).astype(jnp.int32)
    fetch = pltpu.make_async_copy(bounds, limits, sems.at[5])
    fetch.start()
    tile = (slot - owner * TILES + 1).astype(jnp.float32)
    turned = jnp.concatenate([tile] * (LANES // groups), axis=0).T
    for r in range(groups):
        column = jnp.broadcast_to(turned[:, r : r + 1], (LANES, LANES))
        rows[r * LANES : (r + 1) * LANES, 2 * width + LANES :] = column.astype(jnp.bfloat16)

    total = chosen.shape[0]
    amount = 128
    at = 2 * width // LANES * CAP
    cols[total:, :] = jnp.zeros((CAP, cols.shape[1]), jnp.bfloat16)
    ordered[total:, :] = jnp.zeros((CAP, ordered.shape[1]), jnp.bfloat16)
    copies[2].wait()
    for step in range(total // amount):
        wanted = lax.broadcasted_iota(jnp.int32, (amount, LANES), 0) + step * amount
        picked = jnp.concatenate(
            [one_hot(wanted == place[r : r + 1, :]) for r in range(groups)], axis=1
        )
        here = slice(step * amount, (step + 1) * amount)
        chosen[here, :] = picked
        cols[here, :] = dot(picked, rows[:, 2 * width :]).astype(jnp.bfloat16)
    fetch.wait()
    copies[3].wait()
    copies[4].wait()

    def turn(o):
        window = pl.ds(pl.multiple_of(limits[0, o], ALIGN), CAP)
        part = cols[window, :].astype(jnp.float32)
        turned = part[:, :LANES].T
        turned = jnp.where(core == 0, turned[:HALF], turned[HALF:])
        out_ref[o, at : at + HALF, :] = turned.astype(jnp.bfloat16)
        tiles = part[:, LANES:].T[:8]
        slots = lax.broadcasted_iota(jnp.int32, tiles.shape, 1)
        tiles = jnp.where(slots < limits[0, 64 + o], tiles, 0.0)
        out_ref[o, at + HALF : at + HALF + 8, :] = tiles.astype(jnp.bfloat16)

    amount = 256
    steps = total // amount
    for step in range(steps):
        here = slice(step * amount, (step + 1) * amount)
        got = dot(chosen[here, :], rows[:, : 2 * width])
        ordered[here, :width] = (got[:, :width] * got[:, width:]).astype(jnp.bfloat16)
        ordered[here, width:] = got[:, width:].astype(jnp.bfloat16)
        for o in range(step * owners // steps, (step + 1) * owners // steps):
            turn(o)
    for o in range(owners):
        window = pl.ds(pl.multiple_of(limits[0, o], ALIGN), CAP)
        for b in range(2 * width // LANES):
            out_ref[o, b * CAP : (b + 1) * CAP, :] = ordered[window, b * LANES : (b + 1) * LANES]


def grid_kernel(width, other, in_ref, cols_ref, project_ref, expand_ref, *refs):
    out_ref = refs[-1]
    half = (lax.axis_index("chan") + other) % 2
    senders = in_ref.shape[0]
    blocks = 2 * width // LANES
    at_once = 4
    at = blocks * CAP
    parts = out_ref.shape[0]
    mine = TILES * LANES // parts
    last = width // LANES * mine
    total = None
    for first in range(0, senders, at_once):
        group = range(first, first + at_once)
        spectra = jnp.concatenate(
            [
                jnp.concatenate(
                    [in_ref[s, b * CAP : (b + 1) * CAP, :] for b in range(blocks)], axis=1
                )
                for s in group
            ],
            axis=0,
        )
        columns = []
        for s in group:
            kernel_cols = cols_ref[s]
            tile = in_ref[s, at + HALF : at + HALF + 8, :].astype(jnp.float32)
            pieces = []
            for t in range(TILES):
                here = (tile == float(t + 1)).astype(jnp.float32)
                here = jnp.concatenate([here] * (HALF // 8), axis=0).astype(jnp.bfloat16)
                pieces.append(kernel_cols * here)
            columns.append(jnp.concatenate(pieces, axis=0))
        product = dot(jnp.concatenate(columns, axis=1), spectra)
        total = product if total is None else total + product

    cube = total[:, :width] / (total[:, width:] + 1.0)
    high = cube.astype(jnp.bfloat16)
    low = (cube - high.astype(jnp.float32)).astype(jnp.bfloat16)
    both = dot(high, project_ref[...])
    coef = both[:, :LANES] + (both[:, LANES:] + dot(low, project_ref[:, :LANES]))
    first = coef.astype(jnp.bfloat16).astype(jnp.float32)
    left = coef - first
    second = left.astype(jnp.bfloat16).astype(jnp.float32)
    third = left - second
    group = lax.broadcasted_iota(jnp.int32, coef.shape, 1) // BASIS
    terms = jnp.where(group == 2, third, first)
    terms = jnp.where(jnp.logical_or(group == 1, group == 5), second, terms)
    rest = (cube - dot(terms.astype(jnp.bfloat16), expand_ref[...])).astype(jnp.bfloat16)
    sent = terms.T[:16]
    lane = lax.broadcasted_iota(jnp.int32, (8, LANES), 1)
    for at_pixel in range(0, TILES * HALF, mine):
        c = at_pixel // HALF * (LANES // mine) + half * (HALF // mine) + at_pixel % HALF // mine
        for b in range(width // LANES):
            out_ref[c, b * mine : (b + 1) * mine, :] = rest[
                at_pixel : at_pixel + mine, b * LANES : (b + 1) * LANES
            ]
        here = sent[:, at_pixel // LANES * LANES : at_pixel // LANES * LANES + LANES]
        upper, lower = here[:8], here[8:]
        if at_pixel % LANES:
            upper = pltpu.roll(upper, LANES - at_pixel % LANES, axis=1)
        if at_pixel % LANES != mine:
            lower = pltpu.roll(lower, (LANES + mine - at_pixel % LANES) % LANES, axis=1)
        out_ref[c, last : last + 8, :] = jnp.where(lane < mine, upper, lower).astype(jnp.bfloat16)


def final_kernel(
    width, in_ref, combine_ref, short_ref, coef_hbm, res_hbm, coef_ref, res_ref, sems
):
    parts = in_ref.shape[0]
    mine = res_ref.shape[0]
    last = width // LANES * mine
    upper = jnp.concatenate(
        [in_ref[c, last : last + 8, :].astype(jnp.float32) for c in range(parts)], axis=0
    )
    turned = upper.T
    sent = jnp.concatenate([turned[:mine], turned[mine : 2 * mine]], axis=1).astype(jnp.bfloat16)
    mixed = dot(sent, combine_ref[...])
    size = combine_ref.shape[1] // 3
    mixed = mixed[:, :size] + (mixed[:, size : 2 * size] + mixed[:, 2 * size :])
    coef_ref[...] = mixed[:, parts * 8 :].T[:BASIS]
    copies = [pltpu.make_async_copy(coef_ref, coef_hbm, sems.at[0])]
    copies[0].start()
    turned = mixed[:, : parts * 8]
    high = turned.astype(jnp.bfloat16)
    low = (turned - high.astype(jnp.float32)).astype(jnp.bfloat16)
    owner = lax.broadcasted_iota(jnp.int32, high.shape, 1) // 8
    zero = jnp.zeros_like(high)
    pieces = sems.shape[0] - 1
    for piece in range(pieces):
        group = range(piece * parts // pieces, (piece + 1) * parts // pieces)
        highs = jnp.concatenate([jnp.where(owner == c, high, zero) for c in group], axis=0)
        lows = jnp.concatenate([jnp.where(owner == c, low, zero) for c in group], axis=0)
        added = dot(jnp.concatenate([highs, lows, highs], axis=1), short_ref[...])
        for i, c in enumerate(group):
            rest = jnp.concatenate(
                [in_ref[c, b * mine : (b + 1) * mine, :] for b in range(width // LANES)], axis=1
            ).astype(jnp.float32)
            res_ref[:, c * width : (c + 1) * width] = rest + added[i * mine : (i + 1) * mine]
        lanes = slice(group[0] * width, (group[-1] + 1) * width)
        copies.append(
            pltpu.make_async_copy(
                res_ref.at[:, lanes], res_hbm.at[:, lanes], sems.at[piece + 1]
            )
        )
        copies[-1].start()
    for copy in copies:
        copy.wait()


def per_device(owners, parts, spectra, chan_weight, kernel, tile_map, tile_slot):
    count, width = spectra.shape
    mine = TILES * LANES // parts
    project, expand, combine, short = (jnp.asarray(a) for a in tables(CHANNELS, parts))
    limit = pltpu.CompilerParams(vmem_limit_bytes=40 * 2**20)
    hbm = pl.BlockSpec(memory_space=pltpu.HBM)

    long = 2 * width // LANES * CAP + HALF + 8
    room = count + owners * ALIGN
    packed = pl.pallas_call(
        functools.partial(pack_kernel, owners),
        out_shape=jax.ShapeDtypeStruct((owners, long, LANES), jnp.bfloat16),
        in_specs=[hbm] * 5,
        scratch_shapes=[
            pltpu.VMEM((1, tile_slot.shape[0]), jnp.int32),
            pltpu.VMEM((count // LANES, LANES), jnp.int32),
            pltpu.VMEM((count, 2 * width + 2 * LANES), jnp.bfloat16),
            pltpu.VMEM((room, count), jnp.bfloat16),
            pltpu.VMEM((room + CAP, 2 * LANES), jnp.bfloat16),
            pltpu.VMEM((room + CAP, 2 * width), jnp.bfloat16),
            pltpu.VMEM((8, LANES), jnp.int32),
            pltpu.SMEM((8, LANES), jnp.int32),
            pltpu.SemaphoreType.DMA((6,)),
        ],
        compiler_params=limit,
    )(
        *[
            pltpu.with_memory_space_constraint(a, pltpu.HBM)
            for a in (
                tile_slot.reshape(1, -1),
                tile_map.reshape(count // LANES, LANES),
                spectra,
                chan_weight,
                kernel,
            )
        ]
    )

    routed = lax.all_to_all(packed, "scan", split_axis=0, concat_axis=0, tiled=True)

    tall = width // LANES * mine + 8
    at = 2 * width // LANES * CAP
    mine_cols = routed[:, at : at + HALF, :]
    other_cols = lax.ppermute(mine_cols, "chan", [(c, c ^ 1) for c in range(parts)])
    whole = jax.ShapeDtypeStruct((parts, tall, LANES), jnp.bfloat16)
    vmem = pl.BlockSpec(memory_space=pltpu.VMEM)
    first = pl.pallas_call(
        functools.partial(grid_kernel, width, 0),
        out_shape=whole,
        in_specs=[vmem] * 4,
        out_specs=vmem,
        compiler_params=limit,
        cost_estimate=pl.CostEstimate(flops=10**9, bytes_accessed=3 * 10**6, transcendentals=0),
    )(routed, mine_cols, project, expand)
    gridded = pl.pallas_call(
        functools.partial(grid_kernel, width, 1),
        out_shape=whole,
        in_specs=[vmem] * 5,
        out_specs=vmem,
        input_output_aliases={4: 0},
        compiler_params=limit,
        cost_estimate=pl.CostEstimate(flops=10**9, bytes_accessed=3 * 10**6, transcendentals=0),
    )(routed, other_cols, project, expand, first)

    rows = lax.all_to_all(gridded, "chan", split_axis=0, concat_axis=0, tiled=True)

    return pl.pallas_call(
        functools.partial(final_kernel, width),
        out_shape=[
            jax.ShapeDtypeStruct((BASIS, mine), jnp.float32),
            jax.ShapeDtypeStruct((mine, CHANNELS), jnp.float32),
        ],
        out_specs=[hbm, hbm],
        scratch_shapes=[
            pltpu.VMEM((BASIS, mine), jnp.float32),
            pltpu.VMEM((mine, CHANNELS), jnp.float32),
            pltpu.SemaphoreType.DMA((1 + 4,)),
        ],
        compiler_params=limit,
    )(rows, combine, short)


def solution(mesh):
    placed = (P("scan", "chan"), P("scan", "chan"), P("scan", None), P("scan"), P())
    return jax.shard_map(
        functools.partial(per_device, mesh.shape["scan"], mesh.shape["chan"]),
        mesh=mesh,
        in_specs=placed,
        out_specs=(P(None, ("scan", "chan")), P(("scan", "chan"), None)),
        check_vma=False,
    )
```

```python
import functools

import jax
import jax.numpy as jnp
import numpy as np
from jax import lax
from jax.experimental import pallas as pl
from jax.experimental.pallas import tpu as pltpu
from jax.sharding import PartitionSpec as P

CHANNELS = 4096
BASIS = 5
CAP = 128
TILES = 4
LANES = 128
ALIGN = 16
HALF = LANES // 2


def orthonormal(abscissa, terms):
    columns = []
    for degree in range(terms):
        column = abscissa**degree
        for earlier in columns:
            column = column - np.sum(earlier * column) * earlier
        columns.append(column / np.sqrt(np.sum(column * column)))
    return np.stack(columns, axis=1)


def split_terms(values, terms):
    left = np.asarray(values, np.float64)
    parts = []
    for _ in range(terms):
        part = left.astype(jnp.bfloat16)
        parts.append(part)
        left = left - part.astype(np.float64)
    return parts


LEFT = (0, 1, 2, 0, 0, 1)
RIGHT = (0, 0, 0, 1, 2, 1)


def tables(channels, parts):
    width = channels // parts
    basis = orthonormal((2.0 * np.arange(channels) + 1.0) / channels - 1.0, BASIS)
    local = orthonormal((2.0 * np.arange(width) + 1.0) / width - 1.0, BASIS)
    mix = np.stack([local.T @ basis[c * width : (c + 1) * width] for c in range(parts)])
    project = np.zeros((width, LANES))
    expand = np.zeros((LANES, width), jnp.bfloat16)
    terms = split_terms(local.T, 3)
    for group, term in enumerate(RIGHT):
        project[:, group * BASIS : (group + 1) * BASIS] = local
        expand[group * BASIS : (group + 1) * BASIS] = terms[term]
    project = np.concatenate(split_terms(project, 2), axis=1)
    combine = np.zeros((parts * 8 + LANES, parts * 16))
    for c in range(parts):
        for copy in range(3):
            at = c * 16 + copy * BASIS
            combine[parts * 8 : parts * 8 + BASIS, at : at + BASIS] = mix[c].T
            combine[c * 8 : c * 8 + BASIS, at : at + BASIS] += np.eye(BASIS)
    for c in range(parts):
        combine[c * 8 : c * 8 + BASIS] -= mix[c] @ combine[parts * 8 : parts * 8 + BASIS]
    combine = combine.reshape(-1, parts, 2, 8).transpose(0, 2, 1, 3).reshape(-1, parts * 16)
    combine = np.concatenate(split_terms(combine.T, 3), axis=0)
    short = np.zeros((parts, 8, width))
    short[:, :BASIS] = local.T
    short = split_terms(short.reshape(parts * 8, width), 2)
    short = np.concatenate([short[0], short[0], short[1]])
    return project, expand, combine, short


def dot(a, b):
    return jnp.dot(a, b, preferred_element_type=jnp.float32)


def one_hot(mask):
    return mask.astype(jnp.float32).astype(jnp.bfloat16)


def pack_kernel(
    owners,
    slot_hbm,
    map_hbm,
    spec_hbm,
    cw_hbm,
    ker_hbm,
    out_ref,
    slot_ref,
    map_ref,
    rows,
    chosen,
    cols,
    ordered,
    bounds,
    limits,
    sems,
):
    core = lax.axis_index("chan") % 2
    groups = map_ref.shape[0]
    width = spec_hbm.shape[1]
    copies = [
        pltpu.make_async_copy(slot_hbm, slot_ref, sems.at[0]),
        pltpu.make_async_copy(map_hbm, map_ref, sems.at[1]),
        pltpu.make_async_copy(ker_hbm, rows.at[:, 2 * width : 2 * width + LANES], sems.at[2]),
        pltpu.make_async_copy(cw_hbm, rows.at[:, width : 2 * width], sems.at[3]),
        pltpu.make_async_copy(spec_hbm, rows.at[:, :width], sems.at[4]),
    ]
    for copy in copies:
        copy.start()
    size = owners * groups
    at0 = lax.broadcasted_iota(jnp.int32, (LANES, LANES), 0)
    at1 = lax.broadcasted_iota(jnp.int32, (LANES, LANES), 1)
    earlier = one_hot(at0 < at1)
    ones = jnp.ones((LANES, LANES), jnp.bfloat16)
    r0 = lax.broadcasted_iota(jnp.int32, (size, size), 0)
    r1 = lax.broadcasted_iota(jnp.int32, (size, size), 1)
    same = r0 // groups == r1 // groups
    above = one_hot(jnp.logical_and(same, r1 < r0))
    before = one_hot(r1 // groups < r0 // groups)
    copies[0].wait()
    copies[1].wait()

    tile_map = map_ref[...]
    table = jnp.concatenate([slot_ref[...], jnp.zeros_like(slot_ref[...])], axis=1)
    table = jnp.broadcast_to(table, tile_map.shape)
    slot = jnp.take_along_axis(table, tile_map, axis=1, mode="promise_in_bounds")
    owner = slot // TILES
    masks = jnp.concatenate(
        [(owner == o).astype(jnp.float32) for o in range(owners)], axis=0
    ).astype(jnp.bfloat16)
    here = dot(masks, ones).astype(jnp.bfloat16)
    rank = dot(masks, earlier) + dot(above, here)
    count = dot(one_hot(same), here)
    room = jnp.floor((count + (ALIGN - 1.0)) * (1.0 / ALIGN)) * (ALIGN / float(groups))
    begin = dot(before, room.astype(jnp.bfloat16))
    rank = rank + begin
    place = jnp.zeros(owner.shape, jnp.float32)
    for o in range(owners):
        place = jnp.where(owner == o, rank[o * groups : (o + 1) * groups], place)
    place = place.astype(jnp.int32)
    table = jnp.where(at0 == at1 * groups, begin, 0.0)
    table = table + jnp.where(at0 == (at1 - 64) * groups, count, 0.0)
    bounds[...] = jnp.broadcast_to(
        jnp.sum(table, axis=0, keepdims=True), bounds.shape
    ).astype(jnp.int32)
    fetch = pltpu.make_async_copy(bounds, limits, sems.at[5])
    fetch.start()
    tile = (slot - owner * TILES + 1).astype(jnp.float32)
    turned = jnp.concatenate([tile] * (LANES // groups), axis=0).T
    for r in range(groups):
        column = jnp.broadcast_to(turned[:, r : r + 1], (LANES, LANES))
        rows[r * LANES : (r + 1) * LANES, 2 * width + LANES :] = column.astype(jnp.bfloat16)

    total = chosen.shape[0]
    amount = 128
    at = 2 * width // LANES * CAP
    cols[total:, :] = jnp.zeros((CAP, cols.shape[1]), jnp.bfloat16)
    ordered[total:, :] = jnp.zeros((CAP, ordered.shape[1]), jnp.bfloat16)
    copies[2].wait()
    for step in range(total // amount):
        wanted = lax.broadcasted_iota(jnp.int32, (amount, LANES), 0) + step * amount
        picked = jnp.concatenate(
            [one_hot(wanted == place[r : r + 1, :]) for r in range(groups)], axis=1
        )
        here = slice(step * amount, (step + 1) * amount)
        chosen[here, :] = picked
        cols[here, :] = dot(picked, rows[:, 2 * width :]).astype(jnp.bfloat16)
    fetch.wait()
    copies[3].wait()
    copies[4].wait()

    def turn(o):
        window = pl.ds(pl.multiple_of(limits[0, o], ALIGN), CAP)
        part = cols[window, :].astype(jnp.float32)
        turned = part[:, :LANES].T
        turned = jnp.where(core == 0, turned[:HALF], turned[HALF:])
        out_ref[o, at : at + HALF, :] = turned.astype(jnp.bfloat16)
        tiles = part[:, LANES:].T[:8]
        slots = lax.broadcasted_iota(jnp.int32, tiles.shape, 1)
        tiles = jnp.where(slots < limits[0, 64 + o], tiles, 0.0)
        out_ref[o, at + HALF : at + HALF + 8, :] = tiles.astype(jnp.bfloat16)

    steps = total // amount
    for step in range(steps):
        here = slice(step * amount, (step + 1) * amount)
        got = dot(chosen[here, :], rows[:, : 2 * width])
        ordered[here, :width] = (got[:, :width] * got[:, width:]).astype(jnp.bfloat16)
        ordered[here, width:] = got[:, width:].astype(jnp.bfloat16)
        for o in range(step * owners // steps, (step + 1) * owners // steps):
            turn(o)
    for o in range(owners):
        window = pl.ds(pl.multiple_of(limits[0, o], ALIGN), CAP)
        for b in range(2 * width // LANES):
            out_ref[o, b * CAP : (b + 1) * CAP, :] = ordered[window, b * LANES : (b + 1) * LANES]


def grid_kernel(width, other, in_ref, cols_ref, project_ref, expand_ref, *refs):
    out_ref = refs[-1]
    half = (lax.axis_index("chan") + other) % 2
    senders = in_ref.shape[0]
    blocks = 2 * width // LANES
    at_once = 4
    at = blocks * CAP
    parts = out_ref.shape[0]
    mine = TILES * LANES // parts
    last = width // LANES * mine
    total = None
    for first in range(0, senders, at_once):
        group = range(first, first + at_once)
        spectra = jnp.concatenate(
            [
                jnp.concatenate(
                    [in_ref[s, b * CAP : (b + 1) * CAP, :] for b in range(blocks)], axis=1
                )
                for s in group
            ],
            axis=0,
        )
        columns = []
        for s in group:
            kernel_cols = cols_ref[s]
            tile = in_ref[s, at + HALF : at + HALF + 8, :].astype(jnp.float32)
            pieces = []
            for t in range(TILES):
                here = (tile == float(t + 1)).astype(jnp.float32)
                here = jnp.concatenate([here] * (HALF // 8), axis=0).astype(jnp.bfloat16)
                pieces.append(kernel_cols * here)
            columns.append(jnp.concatenate(pieces, axis=0))
        product = dot(jnp.concatenate(columns, axis=1), spectra)
        total = product if total is None else total + product

    cube = total[:, :width] / (total[:, width:] + 1.0)
    high = cube.astype(jnp.bfloat16)
    low = (cube - high.astype(jnp.float32)).astype(jnp.bfloat16)
    both = dot(high, project_ref[...])
    coef = both[:, :LANES] + (both[:, LANES:] + dot(low, project_ref[:, :LANES]))
    first = coef.astype(jnp.bfloat16).astype(jnp.float32)
    left = coef - first
    second = left.astype(jnp.bfloat16).astype(jnp.float32)
    third = left - second
    group = lax.broadcasted_iota(jnp.int32, coef.shape, 1) // BASIS
    terms = jnp.where(group == 2, third, first)
    terms = jnp.where(jnp.logical_or(group == 1, group == 5), second, terms)
    rest = (cube - dot(terms.astype(jnp.bfloat16), expand_ref[...])).astype(jnp.bfloat16)
    sent = terms.T[:16]
    lane = lax.broadcasted_iota(jnp.int32, (8, LANES), 1)
    for at_pixel in range(0, TILES * HALF, mine):
        c = at_pixel // HALF * (LANES // mine) + half * (HALF // mine) + at_pixel % HALF // mine
        for b in range(width // LANES):
            out_ref[c, b * mine : (b + 1) * mine, :] = rest[
                at_pixel : at_pixel + mine, b * LANES : (b + 1) * LANES
            ]
        here = sent[:, at_pixel // LANES * LANES : at_pixel // LANES * LANES + LANES]
        upper, lower = here[:8], here[8:]
        if at_pixel % LANES:
            upper = pltpu.roll(upper, LANES - at_pixel % LANES, axis=1)
        if at_pixel % LANES != mine:
            lower = pltpu.roll(lower, (LANES + mine - at_pixel % LANES) % LANES, axis=1)
        out_ref[c, last : last + 8, :] = jnp.where(lane < mine, upper, lower).astype(jnp.bfloat16)


def final_kernel(
    width, in_ref, combine_ref, short_ref, coef_hbm, res_hbm, coef_ref, res_ref, sems
):
    parts = in_ref.shape[0]
    mine = res_ref.shape[0]
    last = width // LANES * mine
    upper = jnp.concatenate(
        [in_ref[c, last : last + 8, :].astype(jnp.float32) for c in range(parts)], axis=0
    )
    turned = upper.T
    sent = jnp.concatenate([turned[:mine], turned[mine : 2 * mine]], axis=1).astype(jnp.bfloat16)
    mixed = dot(jnp.concatenate([sent] * 3, axis=1), combine_ref[...])
    coef_ref[...] = mixed[:, parts * 8 :].T[:BASIS]
    copies = [pltpu.make_async_copy(coef_ref, coef_hbm, sems.at[0])]
    copies[0].start()
    turned = mixed[:, : parts * 8]
    high = turned.astype(jnp.bfloat16)
    low = (turned - high.astype(jnp.float32)).astype(jnp.bfloat16)
    owner = lax.broadcasted_iota(jnp.int32, high.shape, 1) // 8
    zero = jnp.zeros_like(high)
    pieces = sems.shape[0] - 1
    for piece in range(pieces):
        group = range(piece * parts // pieces, (piece + 1) * parts // pieces)
        highs = jnp.concatenate([jnp.where(owner == c, high, zero) for c in group], axis=0)
        lows = jnp.concatenate([jnp.where(owner == c, low, zero) for c in group], axis=0)
        added = dot(jnp.concatenate([highs, lows, highs], axis=1), short_ref[...])
        for i, c in enumerate(group):
            rest = jnp.concatenate(
                [in_ref[c, b * mine : (b + 1) * mine, :] for b in range(width // LANES)], axis=1
            ).astype(jnp.float32)
            res_ref[:, c * width : (c + 1) * width] = rest + added[i * mine : (i + 1) * mine]
        lanes = slice(group[0] * width, (group[-1] + 1) * width)
        copies.append(
            pltpu.make_async_copy(
                res_ref.at[:, lanes], res_hbm.at[:, lanes], sems.at[piece + 1]
            )
        )
        copies[-1].start()
    for copy in copies:
        copy.wait()


def per_device(owners, parts, spectra, chan_weight, kernel, tile_map, tile_slot):
    count, width = spectra.shape
    mine = TILES * LANES // parts
    project, expand, combine, short = (jnp.asarray(a) for a in tables(CHANNELS, parts))
    limit = pltpu.CompilerParams(vmem_limit_bytes=40 * 2**20)
    hbm = pl.BlockSpec(memory_space=pltpu.HBM)

    long = 2 * width // LANES * CAP + HALF + 8
    room = count + owners * ALIGN
    packed = pl.pallas_call(
        functools.partial(pack_kernel, owners),
        out_shape=jax.ShapeDtypeStruct((owners, long, LANES), jnp.bfloat16),
        in_specs=[hbm] * 5,
        scratch_shapes=[
            pltpu.VMEM((1, tile_slot.shape[0]), jnp.int32),
            pltpu.VMEM((count // LANES, LANES), jnp.int32),
            pltpu.VMEM((count, 2 * width + 2 * LANES), jnp.bfloat16),
            pltpu.VMEM((room, count), jnp.bfloat16),
            pltpu.VMEM((room + CAP, 2 * LANES), jnp.bfloat16),
            pltpu.VMEM((room + CAP, 2 * width), jnp.bfloat16),
            pltpu.VMEM((8, LANES), jnp.int32),
            pltpu.SMEM((8, LANES), jnp.int32),
            pltpu.SemaphoreType.DMA((6,)),
        ],
        compiler_params=limit,
    )(
        *[
            pltpu.with_memory_space_constraint(a, pltpu.HBM)
            for a in (
                tile_slot.reshape(1, -1),
                tile_map.reshape(count // LANES, LANES),
                spectra,
                chan_weight,
                kernel,
            )
        ]
    )

    routed = lax.all_to_all(packed, "scan", split_axis=0, concat_axis=0, tiled=True)

    tall = width // LANES * mine + 8
    at = 2 * width // LANES * CAP
    mine_cols = routed[:, at : at + HALF, :]
    other_cols = lax.ppermute(mine_cols, "chan", [(c, c ^ 1) for c in range(parts)])
    whole = jax.ShapeDtypeStruct((parts, tall, LANES), jnp.bfloat16)
    vmem = pl.BlockSpec(memory_space=pltpu.VMEM)
    first = pl.pallas_call(
        functools.partial(grid_kernel, width, 0),
        out_shape=whole,
        in_specs=[vmem] * 4,
        out_specs=vmem,
        compiler_params=limit,
        cost_estimate=pl.CostEstimate(flops=10**9, bytes_accessed=3 * 10**6, transcendentals=0),
    )(routed, mine_cols, project, expand)
    gridded = pl.pallas_call(
        functools.partial(grid_kernel, width, 1),
        out_shape=whole,
        in_specs=[vmem] * 5,
        out_specs=vmem,
        input_output_aliases={4: 0},
        compiler_params=limit,
        cost_estimate=pl.CostEstimate(flops=10**9, bytes_accessed=3 * 10**6, transcendentals=0),
    )(routed, other_cols, project, expand, first)

    rows = lax.all_to_all(gridded, "chan", split_axis=0, concat_axis=0, tiled=True)

    return pl.pallas_call(
        functools.partial(final_kernel, width),
        out_shape=[
            jax.ShapeDtypeStruct((BASIS, mine), jnp.float32),
            jax.ShapeDtypeStruct((mine, CHANNELS), jnp.float32),
        ],
        out_specs=[hbm, hbm],
        scratch_shapes=[
            pltpu.VMEM((BASIS, mine), jnp.float32),
            pltpu.VMEM((mine, CHANNELS), jnp.float32),
            pltpu.SemaphoreType.DMA((1 + 4,)),
        ],
        compiler_params=limit,
    )(rows, combine, short)


def solution(mesh):
    placed = (P("scan", "chan"), P("scan", "chan"), P("scan", None), P("scan"), P())
    return jax.shard_map(
        functools.partial(per_device, mesh.shape["scan"], mesh.shape["chan"]),
        mesh=mesh,
        in_specs=placed,
        out_specs=(P(None, ("scan", "chan")), P(("scan", "chan"), None)),
        check_vma=False,
    )
```
